256 devices in a mesh: row: 8 (over x, core), col: 8 (over z_lo, y), fiber: 4 (over z_hi).
Axes of the slice: x: 4, y: 4, z: 8 (z_hi: 4, z_lo: 2; z = z_hi * 2 + z_lo), core: 2. Of those that a mesh axis runs over, the one named last changes fastest.
Arguments:
- a_tiles: bfloat16 [64, 192, 128, 128], P('row', ('col', 'fiber'))
- a_cols: int32 [64, 192], P('row', ('col', 'fiber')), may hold values from 0 to 2047, as said below
- a_count: int32 [64, 32], P('row', ('col', 'fiber')), may hold values from 1 to 6, as said below
- b_tiles: bfloat16 [2048, 8, 128, 128], P(('row', 'fiber'), 'col'), may hold values from 0 to 1
- b_cols: int32 [2048, 8], P(('row', 'fiber'), 'col'), may hold values from 0 to 127, as said below
Outputs:
- normalized: float32 [64, 128, 128, 128], P(('row', 'fiber'), 'col')
The draws below stay inside these ranges and needn't reach their ends.
Inputs may be any that keep to these rules, and one draw needn't show every extreme that they name: `a_cols`: a slot in part p of dimension 1 (p = s // 6) holds an inner tile index k with (k // 64) % 4 == p % 4. `a_count`: slots at or beyond the count hold no part of the matrix; some tile row has all slots live in every part. b_cols[k, c] lies in column block c, from c * 16 to (c + 1) * 16 - 1.
All inputs are finite; a program needn't handle non-finite values.
Results may differ from the reference program's by a relative error of at most 0.0003.
Values may be sent and summed in bfloat16 or wider, within the bound.
A program may use at most 128 MiB of HBM per device.

```python
import jax
import jax.numpy as jnp
from jax import lax

TILE = 128
KT = 2048
PT = 128
ASLOTS = 6
MT = 64
N_ROW = 8
N_COL = 8
N_FIBER = 4


def draw_a_tiles(key, part):
    key = jax.random.fold_in(key, 11)
    first_key, second_key = jax.random.split(key)
    shape = (MT, N_COL * N_FIBER * ASLOTS, TILE, TILE)
    rising = 1.0 + 2.0 * jnp.arange(MT, dtype=jnp.float32) / max(MT - 1, 1)
    spread = jax.random.uniform(second_key, shape[:2], jnp.float32, -1.15, 1.15)
    factor = rising[:, None] * jnp.exp(spread)
    entries = jax.random.uniform(first_key, shape, jnp.float32, 0.0, 1.0)
    return (entries * factor[:, :, None, None]).astype(jnp.bfloat16)


def draw_a_cols(key, part):
    key = jax.random.fold_in(key, 23)
    first_key, second_key = jax.random.split(key)
    slot_total = N_COL * N_FIBER * ASLOTS
    block_rows = KT // (N_ROW * N_FIBER)
    outer = jax.random.randint(first_key, (MT, slot_total), 0, N_ROW, dtype=jnp.int32)
    inner = jax.random.randint(second_key, (MT, slot_total), 0, block_rows, dtype=jnp.int32)
    layer_ids = jnp.arange(slot_total, dtype=jnp.int32) // ASLOTS % N_FIBER
    return ((outer * N_FIBER + layer_ids[None, :]) * block_rows + inner).astype(jnp.int32)


def draw_a_count(key, part):
    key = jax.random.fold_in(key, 37)
    first_key, second_key, third_key = jax.random.split(key, 3)
    level = jax.random.randint(first_key, (MT, 1), 0, 4, dtype=jnp.int32)
    lowest = 1 + level * (ASLOTS // 4)
    counts = jax.random.randint(second_key, (MT, N_COL * N_FIBER), lowest, ASLOTS + 1, dtype=jnp.int32)
    full_row = jax.random.randint(third_key, (), 0, MT, dtype=jnp.int32)
    row_ids = jnp.arange(MT, dtype=jnp.int32)[:, None]
    return jnp.where(row_ids == full_row, ASLOTS, counts).astype(jnp.int32)


def draw_b_cols(key, part):
    key = jax.random.fold_in(key, 41)
    block_cols = PT // N_COL
    picked = jax.random.randint(key, (KT, N_COL), 0, block_cols, dtype=jnp.int32)
    return (jnp.arange(N_COL, dtype=jnp.int32)[None, :] * block_cols + picked).astype(jnp.int32)


def level_of(rng, shape, cuts, least, top_value):
    def one(axis_at, parts):
        steps = jax.random.uniform(jax.random.fold_in(jax.random.fold_in(rng, 6), axis_at), (parts,), jnp.float32, least / len(cuts), top_value / len(cuts))
        return jnp.repeat(jnp.exp(steps), shape[axis_at] // parts).reshape((-1,) + (1,) * (len(shape) - axis_at - 1))

    gain = one(*cuts[0])
    for cut in cuts[1:]:
        gain = gain * one(*cut)
    return gain


def setup_inputs(seed: int = 0) -> dict:
    seeds = jax.random.split(jax.random.key(seed), 6)
    return {
        "a_tiles": draw_a_tiles(jax.random.fold_in(seeds[5], 71), 0),
        "a_cols": draw_a_cols(jax.random.fold_in(seeds[5], 71), 0),
        "a_count": draw_a_count(jax.random.fold_in(seeds[5], 71), 0),
        "b_tiles": jnp.clip(1.0 * jax.random.uniform(seeds[3], (KT, N_COL, TILE, TILE), jnp.float32) ** level_of(seeds[3], (KT, N_COL, TILE, TILE), ((0, 32), (1, 8)), -0.2, 0.2), 0.0, 1.0).astype(jnp.bfloat16),
        "b_cols": draw_b_cols(jax.random.fold_in(seeds[5], 71), 0),
    }


epsilon = 1e-6


def reference(a_tiles, a_cols, a_count, b_tiles, b_cols):
    slot_total = a_tiles.shape[1]
    position = jnp.arange(slot_total) % ASLOTS
    slot_live = (position[None, :] < jnp.repeat(a_count, ASLOTS, axis=1)).astype(jnp.float32)

    def one_row(inputs):
        tile_set, tile_cols, live_row = inputs
        partner = b_tiles[tile_cols].astype(jnp.float32)
        products = jnp.einsum("sab,snbc->snac", tile_set.astype(jnp.float32), partner, precision=lax.Precision.HIGHEST)
        products = products * live_row[:, None, None, None]
        target = b_cols[tile_cols].reshape(-1)
        zero_tiles = jnp.zeros((PT, TILE, TILE), jnp.float32)
        return zero_tiles.at[target].add(products.reshape(-1, TILE, TILE))

    squared = lax.map(one_row, (a_tiles, a_cols, slot_live))
    inflated = squared * squared
    column_total = jnp.sum(inflated, axis=(0, 2))
    return inflated * ((MT * TILE) / (column_total + epsilon))[None, :, None, :]
```

```python
import functools

import jax
import jax.numpy as jnp
from jax import lax
from jax.experimental import pallas as pl
from jax.experimental.pallas import tpu as pltpu
from jax.sharding import PartitionSpec as P

MESH = pl.DeviceIdType.MESH
PT = 128
ASLOTS = 6
SLOTS8 = 8
TILE = 128
epsilon = 1e-06
F32 = jnp.float32
PIECES = 4
TOP = 32767.0


def kernel(total_rows, am_ref, bm_ref, a_ref, b_ref, out_ref, pa, pb, ma, mb, meta_v, meta_s, sums, cq_s, cs_s, cq_r, cs_r, own, t1, t2, gains,
           loc_sem, ma_sem, mb_sem, ao_sem, ap_sem, af_sem, bo_sem, bk_sem, bf_sem, cq_sem, cs_sem, t1_sem, t2_sem):
    r, c, f = lax.axis_index("row"), lax.axis_index("col"), lax.axis_index("fiber")
    x, k = r // 2, r % 2
    zl, y = c // 4, c % 4

    def rdev(rr):
        return (rr, c, f)

    def cdev(cc):
        return (r, cc, f)

    def fdev(ff):
        return (r, c, ff)

    def rid(dx, kk):
        return ((x + dx + 4) % 4) * 2 + kk

    def cid(dy, zz):
        return zz * 4 + (y + dy + 4) % 4

    XP, XM, KP = rdev(rid(1, k)), rdev(rid(-1, k)), rdev(rid(0, 1 - k))
    YP, YM, ZP = cdev(cid(1, zl)), cdev(cid(-1, zl)), cdev(cid(0, 1 - zl))
    FP, FM = fdev((f + 1) % 4), fdev((f + 3) % 4)
    row_peers = [rdev((r + d) % 8) for d in range(1, 8)]
    col_peers = [cdev((c + d) % 8) for d in range(1, 8)]
    fib_peers = [fdev((f + d) % 4) for d in range(1, 4)]

    barrier = pltpu.get_barrier_semaphore()
    for peer in row_peers + col_peers + fib_peers:
        pl.semaphore_signal(barrier, inc=1, device_id=peer, device_id_type=MESH)

    locals_ = [
        pltpu.make_async_copy(am_ref, ma.at[c], loc_sem.at[0]),
        pltpu.make_async_copy(bm_ref, mb.at[r], loc_sem.at[1]),
        pltpu.make_async_copy(a_ref, pa.at[:, c], loc_sem.at[2]),
        pltpu.make_async_copy(b_ref, pb.at[pl.ds(r * 64, 64)], loc_sem.at[3]),
    ]
    for copy in locals_:
        copy.start()
    sums[0] = jnp.zeros((TILE, TILE), F32)
    pl.semaphore_wait(barrier, len(row_peers) + len(col_peers) + len(fib_peers))

    started = []

    def send(src, dst, sem, at, device):
        copy = pltpu.make_async_remote_copy(
            src_ref=src, dst_ref=dst, send_sem=sem.at[(0,) + at], recv_sem=sem.at[(1,) + at], device_id=device, device_id_type=MESH
        )
        copy.start()
        started.append(copy)

    def arrive(dst, sem, at):
        pltpu.make_async_remote_copy(
            src_ref=dst, dst_ref=dst, send_sem=sem.at[(0,) + at], recv_sem=sem.at[(1,) + at], device_id=KP, device_id_type=MESH
        ).wait_recv()

    for d in range(1, 8):
        send(am_ref, ma.at[c], ma_sem, (d - 1,), col_peers[d - 1])
        send(bm_ref, mb.at[r], mb_sem, (d - 1,), row_peers[d - 1])

    step = 64 // PIECES

    def b_at(block, q):
        return pb.at[pl.ds(block * 64 + q * step, step)]

    for q in range(PIECES):
        src = b_ref.at[pl.ds(q * step, step)]
        send(src, b_at(r, q), bo_sem, (q, 1), XP)
        send(src, b_at(r, q), bo_sem, (q, 2), XM)
        send(src, b_at(r, q), bo_sem, (q, 0), KP)

    def b_near(q):
        block = rid(-1, k)
        arrive(b_at(block, q), bo_sem, (q, 1))
        if q < PIECES // 2:
            send(b_at(block, q), b_at(block, q), bf_sem, (q,), XP)
        send(b_at(block, q), b_at(block, q), bk_sem, (q, 0), KP)
        block = rid(1, k)
        arrive(b_at(block, q), bo_sem, (q, 2))
        if q >= PIECES // 2:
            send(b_at(block, q), b_at(block, q), bf_sem, (q,), XM)
        send(b_at(block, q), b_at(block, q), bk_sem, (q, 1), KP)

    def b_far(q):
        block = rid(2, k)
        arrive(b_at(block, q), bf_sem, (q,))
        send(b_at(block, q), b_at(block, q), bk_sem, (q, 2), KP)

    def b_done():
        for q in range(PIECES):
            arrive(b_at(rid(0, 1 - k), q), bo_sem, (q, 0))
            arrive(b_at(rid(-1, 1 - k), q), bk_sem, (q, 0))
            arrive(b_at(rid(1, 1 - k), q), bk_sem, (q, 1))
            arrive(b_at(rid(2, 1 - k), q), bk_sem, (q, 2))
        locals_[3].wait()

    plus, minus, far = (f + 1) % 4, (f + 3) % 4, (f + 2) % 4
    rows = [far * 2, far * 2 + 1, plus * 2 + 1, minus * 2, plus * 2, minus * 2 + 1, f * 2, f * 2 + 1]

    def a_own(n):
        row = rows[n]
        for way, device in enumerate((ZP, YP, YM)):
            send(a_ref.at[row], pa.at[row, c], ao_sem, (n, way), device)

    def a_half(n, block, half, way, device):
        part = pa.at[rows[n], block, pl.ds(half * 3, 3)]
        send(part, part, af_sem, (n, way), device)

    def a_near(n):
        row = rows[n]
        block = cid(0, 1 - zl)
        arrive(pa.at[row, block], ao_sem, (n, 0))
        for way, device in enumerate((YP, YM)):
            send(pa.at[row, block], pa.at[row, block], ap_sem, (n, way), device)
        if n + 2 < 8:
            a_own(n + 2)
        arrive(pa.at[row, cid(-1, zl)], ao_sem, (n, 1))
        a_half(n, cid(-1, zl), 0, 0, YP)
        arrive(pa.at[row, cid(1, zl)], ao_sem, (n, 2))
        a_half(n, cid(1, zl), 1, 1, YM)

    def a_pair(n):
        row = rows[n]
        arrive(pa.at[row, cid(-1, 1 - zl)], ap_sem, (n, 0))
        a_half(n, cid(-1, 1 - zl), 0, 2, YP)
        arrive(pa.at[row, cid(1, 1 - zl)], ap_sem, (n, 1))
        a_half(n, cid(1, 1 - zl), 1, 3, YM)

    def a_done(n):
        row = rows[n]
        for way, (zz, half) in enumerate(((zl, 0), (zl, 1), (1 - zl, 0), (1 - zl, 1))):
            arrive(pa.at[row, cid(2, zz), pl.ds(half * 3, 3)], af_sem, (n, way))

    def index_tables():
        locals_[0].wait()
        locals_[1].wait()
        for d in range(1, 8):
            arrive(ma.at[(c + 8 - d) % 8], ma_sem, (d - 1,))
            arrive(mb.at[(r + 8 - d) % 8], mb_sem, (d - 1,))
        lane = lax.broadcasted_iota(jnp.int32, (64, TILE), 1)
        slot = lax.broadcasted_iota(jnp.int32, (64, TILE), 0)

        def one_row(i, carry):
            place = ma[:, i].reshape(64, TILE)
            target = jnp.zeros((64, TILE), jnp.int32)
            for q in range(8):
                hit = (place == lane + q * 64) & (lane < 64)
                target = target + jnp.where(hit, mb[q, 0:1, :], 0)
            target = jnp.sum(target, axis=1, keepdims=True)
            target = jnp.broadcast_to(target, (64, TILE))
            here = slot == lane
            target_l = jnp.sum(jnp.where(here, target, 0), axis=0, keepdims=True)
            place_l = jnp.sum(jnp.where(here, jnp.maximum(place, 0), 0), axis=0, keepdims=True)
            same = (target == target_l) & (slot < lane) & (target > 0)
            prev = jnp.max(jnp.where(same, slot + 1, 0), axis=0, keepdims=True)
            last = jnp.max(jnp.where(target == lane + 1, slot + 1, 0), axis=0, keepdims=True)
            meta_v[i, 0:1, :] = place_l
            meta_v[i, 1:2, :] = prev
            meta_v[i, 2:3, :] = last
            return carry

        lax.fori_loop(0, 8, one_row, 0)
        copy = pltpu.make_async_copy(meta_v, meta_s, loc_sem.at[4])
        copy.start()
        copy.wait()
        locals_[2].wait()

    def products(n):
        row = rows[n]

        def one_part(p, carry):
            for e in range(ASLOTS):
                t = p * SLOTS8 + e
                product = jnp.dot(pa[row, p, e], pb[meta_s[row, 0, t]], preferred_element_type=F32)
                sums[1 + t] = product + sums[meta_s[row, 1, t]]
            return carry

        lax.fori_loop(0, 8, one_part, 0)

    def decoded(at, j):
        return cq_r[at, j].astype(jnp.int32).astype(F32) * cs_r[at, pl.ds(j, 1), :]

    def emit(n, at, device, add=None):
        row = rows[n]

        def one_tile(j, carry):
            value = sums[meta_s[row, 2, j]]
            if add is not None:
                value = value + decoded(add, j)
            top = jnp.max(jnp.abs(value), axis=0, keepdims=True)
            gain = jnp.where(top > 1e-30, TOP / jnp.maximum(top, 1e-30), 0.0)
            cs_s[at, pl.ds(j, 1), :] = top * (1.0 / TOP)
            cq_s[at, j] = jnp.floor(value * gain + 0.5).astype(jnp.int32).astype(jnp.int16)
            return carry

        lax.fori_loop(0, 16, one_tile, 0)
        send(cs_s.at[at], cs_r.at[at], cs_sem, (at,), device)
        send(cq_s.at[at], cq_r.at[at], cq_sem, (at,), device)

    def c_arrive(at):
        arrive(cs_r.at[at], cs_sem, (at,))
        arrive(cq_r.at[at], cq_sem, (at,))

    def keep(n, half):
        row = rows[n]

        def one_tile(j, carry):
            own[half, j] = sums[meta_s[row, 2, j]]
            return carry

        lax.fori_loop(0, 16, one_tile, 0)

    a_own(0)
    a_own(1)
    a_near(0)
    index_tables()
    b_near(0)
    a_near(1)
    a_pair(0)
    b_near(1)
    a_near(2)
    a_pair(1)
    b_near(2)
    a_near(3)
    a_pair(2)
    b_near(3)
    a_near(4)
    a_pair(3)
    b_far(0)
    b_far(2)
    a_near(5)
    a_pair(4)
    b_far(1)
    b_far(3)
    b_done()
    a_done(0)
    products(0)
    emit(0, 0, FP)
    a_near(6)
    a_pair(5)
    a_done(1)
    products(1)
    emit(1, 1, FM)
    a_done(2)
    products(2)
    emit(2, 3, FP)
    a_near(7)
    a_pair(6)
    a_done(3)
    products(3)
    emit(3, 4, FM)
    a_done(4)
    products(4)
    c_arrive(0)
    emit(4, 2, FP, add=0)
    a_pair(7)
    a_done(5)
    products(5)
    c_arrive(1)
    emit(5, 5, FM, add=1)
    a_done(6)
    products(6)
    keep(6, 0)
    a_done(7)
    products(7)
    keep(7, 1)
    for at in (3, 4, 2, 5):
        c_arrive(at)

    def square(j, carry):
        total = jnp.zeros((1, TILE), F32)
        for half in range(2):
            value = own[half, j] + decoded(2 + half, j) + decoded(4 + half, j)
            value = value * value
            own[half, j] = value
            total = total + jnp.sum(value, axis=0, keepdims=True)
        t1[r, pl.ds(j, 1), :] = total
        return carry

    lax.fori_loop(0, 16, square, 0)
    for d in range(1, 8):
        send(t1.at[r], t1.at[r], t1_sem, (d - 1,), row_peers[d - 1])
    for d in range(1, 8):
        arrive(t1.at[(r + 8 - d) % 8], t1_sem, (d - 1,))
    t2[f] = jnp.sum(t1[...], axis=0)
    for d in range(1, 4):
        send(t2.at[f], t2.at[f], t2_sem, (d - 1,), fib_peers[d - 1])
    for d in range(1, 4):
        arrive(t2.at[(f + 4 - d) % 4], t2_sem, (d - 1,))
    gains[...] = total_rows / (jnp.sum(t2[...], axis=0) + epsilon)

    def scale(j, carry):
        gain = gains[pl.ds(j, 1), :]
        for half in range(2):
            out_ref[half, j] = own[half, j] * gain
        return carry

    lax.fori_loop(0, 16, scale, 0)
    for copy in started:
        copy.wait_send()


def on_device(a_tiles, a_cols, a_count, b_tiles, b_cols):
    fibers = lax.axis_size("fiber")
    block_rows = b_tiles.shape[0]
    col_offset = lax.axis_index("col") * (PT // lax.axis_size("col"))
    place = a_cols // (block_rows * fibers) * block_rows + a_cols % block_rows
    place = jnp.where(jnp.arange(ASLOTS)[None, :] < a_count, place, -1)
    place = jnp.pad(place, ((0, 0), (0, SLOTS8 - ASLOTS)), constant_values=-1)
    place = jnp.broadcast_to(place[:, :, None], place.shape + (TILE,))
    target = jnp.pad(b_cols[:, 0] - col_offset + 1, (0, TILE - block_rows))
    target = jnp.broadcast_to(target[None, :], (8, TILE))
    total_rows = 8 * lax.axis_size("row") * TILE
    dma = pltpu.SemaphoreType.DMA
    any_ = pl.BlockSpec(memory_space=pl.ANY)
    return pl.pallas_call(
        functools.partial(kernel, total_rows),
        out_shape=jax.ShapeDtypeStruct((2, 16, TILE, TILE), F32),
        in_specs=[any_] * 4,
        out_specs=pl.BlockSpec(memory_space=pltpu.VMEM),
        scratch_shapes=[
            pltpu.VMEM((8, 8, ASLOTS, TILE, TILE), jnp.bfloat16),
            pltpu.VMEM((512, TILE, TILE), jnp.bfloat16),
            pltpu.VMEM((8, 8, SLOTS8, TILE), jnp.int32),
            pltpu.VMEM((8, 8, TILE), jnp.int32),
            pltpu.VMEM((8, 8, TILE), jnp.int32),
            pltpu.SMEM((8, 8, TILE), jnp.int32),
            pltpu.VMEM((65, TILE, TILE), F32),
            pltpu.VMEM((6, 16, TILE, TILE), jnp.int16),
            pltpu.VMEM((6, 16, TILE), F32),
            pltpu.VMEM((6, 16, TILE, TILE), jnp.int16),
            pltpu.VMEM((6, 16, TILE), F32),
            pltpu.VMEM((2, 16, TILE, TILE), F32),
            pltpu.VMEM((8, 16, TILE), F32),
            pltpu.VMEM((4, 16, TILE), F32),
            pltpu.VMEM((16, TILE), F32),
            dma((5,)),
            dma((2, 7)),
            dma((2, 7)),
            dma((2, 8, 3)),
            dma((2, 8, 2)),
            dma((2, 8, 4)),
            dma((2, PIECES, 3)),
            dma((2, PIECES, 3)),
            dma((2, PIECES)),
            dma((2, 6)),
            dma((2, 6)),
            dma((2, 7)),
            dma((2, 3)),
        ],
        compiler_params=pltpu.CompilerParams(collective_id=0, has_side_effects=True, vmem_limit_bytes=60 * 1024 * 1024),
    )(place, target, a_tiles, b_tiles.reshape(block_rows, TILE, TILE))


def solution(mesh):
    placed = (
        P("row", ("col", "fiber"), None, None),
        P("row", ("col", "fiber")),
        P("row", ("col", "fiber")),
        P(("row", "fiber"), "col", None, None),
        P(("row", "fiber"), "col"),
    )
    return jax.shard_map(
        on_device,
        mesh=mesh,
        in_specs=placed,
        out_specs=P(("row", "fiber"), "col", None, None),
        check_vma=False,
    )
```

```python
import functools

import jax
import jax.numpy as jnp
from jax import lax
from jax.experimental import pallas as pl
from jax.experimental.pallas import tpu as pltpu
from jax.sharding import PartitionSpec as P

MESH = pl.DeviceIdType.MESH
PT = 128
ASLOTS = 6
SLOTS8 = 8
TILE = 128
epsilon = 1e-06
F32 = jnp.float32
PIECES = 4
TOP = 32767.0


def kernel(total_rows, meta_ref, a_ref, b_ref, out_ref, gain_ref, pa, pb0, pb1, raw, ma, mb, meta_v, meta_s, sums, cq_s, cs_s, cq_r, cs_r, own, t1, t2,
           loc_sem, ma_sem, mb_sem, ao_sem, ap_sem, af_sem, bo_sem, bk_sem, bf_sem, cq_sem, cs_sem, t1_sem, t2_sem):
    r, c, f = lax.axis_index("row"), lax.axis_index("col"), lax.axis_index("fiber")
    x, k = r // 2, r % 2
    zl, y = c // 4, c % 4
    pb = (pb0, pb1)

    def rdev(rr):
        return (rr, c, f)

    def cdev(cc):
        return (r, cc, f)

    def fdev(ff):
        return (r, c, ff)

    def rid(dx, kk):
        return ((x + dx + 4) % 4) * 2 + kk

    def cid(dy, zz):
        return zz * 4 + (y + dy + 4) % 4

    XP, XM, KP = rdev(rid(1, k)), rdev(rid(-1, k)), rdev(rid(0, 1 - k))
    YP, YM, ZP = cdev(cid(1, zl)), cdev(cid(-1, zl)), cdev(cid(0, 1 - zl))
    FP, FM = fdev((f + 1) % 4), fdev((f + 3) % 4)
    row_peers = [rdev((r + d) % 8) for d in range(1, 8)]
    col_peers = [cdev((c + d) % 8) for d in range(1, 8)]
    fib_peers = [fdev((f + d) % 4) for d in range(1, 4)]

    barrier = pltpu.get_barrier_semaphore()
    for peer in row_peers + col_peers + fib_peers:
        pl.semaphore_signal(barrier, inc=1, device_id=peer, device_id_type=MESH)

    am_ref, bm_ref = meta_ref.at[pl.ds(0, 8)], meta_ref.at[pl.ds(8, 8)]
    locals_ = [
        pltpu.make_async_copy(am_ref, ma.at[c], loc_sem.at[0]),
        pltpu.make_async_copy(bm_ref, mb.at[r], loc_sem.at[1]),
        pltpu.make_async_copy(a_ref, pa.at[:, c], loc_sem.at[2]),
        pltpu.make_async_copy(b_ref, raw, loc_sem.at[3]),
    ]
    for n in (3, 0, 1, 2):
        locals_[n].start()
    sums[0] = jnp.zeros((TILE, TILE), F32)
    low = lax.broadcasted_iota(jnp.int32, (1, TILE), 1) < TILE // 2

    def swapped(value):
        return pltpu.roll(value, TILE // 2, 1)

    def pack(h, q):
        def one_pair(n, carry):
            first, second = raw[2 * n].astype(F32), raw[2 * n + 1].astype(F32)
            if h == 0:
                pair = jnp.where(low, first, swapped(second))
            else:
                pair = jnp.where(low, swapped(first), second)
            pb[h][r * 32 + n] = pair.astype(jnp.bfloat16)
            return carry

        lax.fori_loop(q * (32 // PIECES), (q + 1) * (32 // PIECES), one_pair, 0)

    pl.semaphore_wait(barrier, len(row_peers) + len(col_peers) + len(fib_peers))

    started = []

    def send(src, dst, sem, at, device):
        copy = pltpu.make_async_remote_copy(
            src_ref=src, dst_ref=dst, send_sem=sem.at[(0,) + at], recv_sem=sem.at[(1,) + at], device_id=device, device_id_type=MESH
        )
        copy.start()
        started.append(copy)

    def arrive(dst, sem, at):
        pltpu.make_async_remote_copy(
            src_ref=dst, dst_ref=dst, send_sem=sem.at[(0,) + at], recv_sem=sem.at[(1,) + at], device_id=KP, device_id_type=MESH
        ).wait_recv()

    step = 32 // PIECES

    def b_at(h, block, q):
        return pb[h].at[pl.ds(block * 32 + q * step, step)]

    def b_own(h, q):
        part = b_at(h, r, q)
        send(part, part, bo_sem, (h, q, 1), XP)
        send(part, part, bo_sem, (h, q, 2), XM)
        send(part, part, bo_sem, (h, q, 0), KP)

    def b_near(h, q):
        part = b_at(h, rid(-1, k), q)
        arrive(part, bo_sem, (h, q, 1))
        if q < PIECES // 2:
            send(part, part, bf_sem, (h, q), XP)
        send(part, part, bk_sem, (h, q, 0), KP)
        part = b_at(h, rid(1, k), q)
        arrive(part, bo_sem, (h, q, 2))
        if q >= PIECES // 2:
            send(part, part, bf_sem, (h, q), XM)
        send(part, part, bk_sem, (h, q, 1), KP)

    def b_far(h, q):
        part = b_at(h, rid(2, k), q)
        arrive(part, bf_sem, (h, q))
        send(part, part, bk_sem, (h, q, 2), KP)

    def b_done(h):
        for q in range(PIECES):
            arrive(b_at(h, rid(0, 1 - k), q), bo_sem, (h, q, 0))
            arrive(b_at(h, rid(-1, 1 - k), q), bk_sem, (h, q, 0))
            arrive(b_at(h, rid(1, 1 - k), q), bk_sem, (h, q, 1))
            arrive(b_at(h, rid(2, 1 - k), q), bk_sem, (h, q, 2))

    plus, minus, far = (f + 1) % 4, (f + 3) % 4, (f + 2) % 4
    rows = [far * 2, far * 2 + 1, plus * 2 + 1, minus * 2, plus * 2, minus * 2 + 1, f * 2, f * 2 + 1]

    def a_own(n, ways):
        row = rows[n]
        for way, device in enumerate((ZP, YP, YM)):
            if way in ways:
                send(a_ref.at[row], pa.at[row, c], ao_sem, (n, way), device)

    def a_half(n, block, half, way, device):
        part = pa.at[rows[n], block, pl.ds(half * 3, 3)]
        send(part, part, af_sem, (n, way), device)

    def a_near(n):
        row = rows[n]
        block = cid(0, 1 - zl)
        arrive(pa.at[row, block], ao_sem, (n, 0))
        for way, device in enumerate((YP, YM)):
            send(pa.at[row, block], pa.at[row, block], ap_sem, (n, way), device)
        if n + 3 < 8:
            a_own(n + 3, (0,))
        arrive(pa.at[row, cid(-1, zl)], ao_sem, (n, 1))
        a_half(n, cid(-1, zl), 0, 0, YP)
        arrive(pa.at[row, cid(1, zl)], ao_sem, (n, 2))
        a_half(n, cid(1, zl), 1, 1, YM)

    def a_pair(n):
        row = rows[n]
        arrive(pa.at[row, cid(-1, 1 - zl)], ap_sem, (n, 0))
        a_half(n, cid(-1, 1 - zl), 0, 2, YP)
        arrive(pa.at[row, cid(1, 1 - zl)], ap_sem, (n, 1))
        a_half(n, cid(1, 1 - zl), 1, 3, YM)
        if n + 2 < 8:
            a_own(n + 2, (1, 2))

    def a_done(n):
        row = rows[n]
        for way, (zz, half) in enumerate(((zl, 0), (zl, 1), (1 - zl, 0), (1 - zl, 1))):
            arrive(pa.at[row, cid(2, zz), pl.ds(half * 3, 3)], af_sem, (n, way))

    def index_tables():
        for d in range(1, 8):
            arrive(ma.at[(c + 8 - d) % 8], ma_sem, (d - 1,))
            arrive(mb.at[(r + 8 - d) % 8], mb_sem, (d - 1,))
        lane = lax.broadcasted_iota(jnp.int32, (64, TILE), 1)
        slot = lax.broadcasted_iota(jnp.int32, (64, TILE), 0)
        lane8 = lax.broadcasted_iota(jnp.int32, (8, TILE), 1)
        slot8 = lax.broadcasted_iota(jnp.int32, (8, TILE), 0)

        def one_row(i, carry):
            place = []
            for p in range(8):
                part = jnp.broadcast_to(ma[p, pl.ds(i, 1), :], (8, TILE))
                part = jnp.sum(jnp.where(slot8 == lane8, part, 0), axis=1, keepdims=True)
                place.append(jnp.broadcast_to(part, (8, TILE)))
            place = jnp.concatenate(place, axis=0)
            target = jnp.zeros((64, TILE), jnp.int32)
            for q in range(8):
                hit = (place == lane + q * 64) & (lane < 64)
                target = target + jnp.where(hit, mb[q, 0:1, :], 0)
            target = jnp.sum(target, axis=1, keepdims=True)
            target = jnp.broadcast_to(target, (64, TILE))
            here = slot == lane
            target_l = jnp.sum(jnp.where(here, target, 0), axis=0, keepdims=True)
            place_l = jnp.sum(jnp.where(here, jnp.maximum(place, 0), 0), axis=0, keepdims=True)
            same = (target == target_l) & (slot < lane) & (target > 0)
            prev = jnp.max(jnp.where(same, slot + 1, 0), axis=0, keepdims=True)
            last = jnp.max(jnp.where(target == lane + 1, slot + 1, 0), axis=0, keepdims=True)
            meta_v[i, 0:1, :] = place_l >> 1
            meta_v[i, 1:2, :] = prev
            meta_v[i, 2:3, :] = last
            meta_v[i, 3:4, :] = place_l & 1
            return carry

        lax.fori_loop(0, 8, one_row, 0)
        copy = pltpu.make_async_copy(meta_v, meta_s, loc_sem.at[4])
        copy.start()
        copy.wait()

    def products(n, h):
        row = rows[n]
        half = lax.broadcasted_iota(jnp.int32, (1, TILE), 1) // (TILE // 2)

        def one_part(p, carry):
            for e in range(ASLOTS):
                t = p * SLOTS8 + e
                product = jnp.dot(pa[row, p, e], pb[h][meta_s[row, 0, t]], preferred_element_type=F32)
                product = jnp.where(half == meta_s[row, 3, t], product, 0.0)
                sums[1 + t] = product + sums[meta_s[row, 1, t]]
            return carry

        lax.fori_loop(0, 8, one_part, 0)

    def total_pair(row, n):
        first, second = sums[meta_s[row, 2, 2 * n]], sums[meta_s[row, 2, 2 * n + 1]]
        return jnp.where(low, first, second) + swapped(jnp.where(low, second, first))

    def decoded(at, n):
        return cq_r[at, n].astype(jnp.int32).astype(F32) * cs_r[at, pl.ds(n, 1), :]

    def emit(n, h, at, device, add=None):
        row = rows[n]
        at = at * 2 + h

        def one_tile(j, carry):
            value = total_pair(row, j)
            if add is not None:
                value = value + decoded(add * 2 + h, j)
            top = jnp.max(jnp.abs(value), axis=0, keepdims=True)
            gain = jnp.where(top > 1e-30, TOP / jnp.maximum(top, 1e-30), 0.0)
            cs_s[at, pl.ds(j, 1), :] = top * (1.0 / TOP)
            cq_s[at, j] = jnp.floor(value * gain + 0.5).astype(jnp.int32).astype(jnp.int16)
            return carry

        lax.fori_loop(0, 8, one_tile, 0)
        send(cs_s.at[at], cs_r.at[at], cs_sem, (at,), device)
        send(cq_s.at[at], cq_r.at[at], cq_sem, (at,), device)

    def c_arrive(at, h):
        at = at * 2 + h
        arrive(cs_r.at[at], cs_sem, (at,))
        arrive(cq_r.at[at], cq_sem, (at,))

    def keep(n, h, half):
        row = rows[n]

        def one_tile(j, carry):
            own[half, h, j] = total_pair(row, j)
            return carry

        lax.fori_loop(0, 8, one_tile, 0)

    def unit(n, h):
        products(n, h)
        if n == 0:
            emit(0, h, 0, FP)
        elif n == 1:
            emit(1, h, 1, FM)
        elif n == 2:
            emit(2, h, 3, FP)
        elif n == 3:
            emit(3, h, 4, FM)
        elif n == 4:
            c_arrive(0, h)
            emit(4, h, 2, FP, add=0)
        elif n == 5:
            c_arrive(1, h)
            emit(5, h, 5, FM, add=1)
        else:
            keep(n, h, n - 6)

    def start():
        for copy in locals_[:2]:
            copy.wait()
        for d in range(1, 8):
            send(ma.at[c], ma.at[c], ma_sem, (d - 1,), col_peers[d - 1])
            send(mb.at[r], mb.at[r], mb_sem, (d - 1,), row_peers[d - 1])
        a_own(0, (0, 1, 2))
        a_own(1, (0, 1, 2))
        a_own(2, (0,))
        locals_[3].wait()
        for q in range(PIECES):
            pack(0, q)
            b_own(0, q)
        for q in range(PIECES):
            pack(1, q)

    start()
    b_near(0, 0)
    a_near(0)
    a_near(1)
    b_near(0, 1)
    a_pair(0)
    index_tables()
    b_near(0, 2)
    a_pair(1)
    b_near(0, 3)
    a_near(2)
    b_far(0, 0)
    b_far(0, 2)
    b_own(1, 0)
    b_far(0, 1)
    b_far(0, 3)
    for q in range(1, PIECES):
        b_own(1, q)
    a_near(3)
    locals_[2].wait()
    b_done(0)
    a_done(0)
    unit(0, 0)
    a_pair(2)
    a_done(1)
    unit(1, 0)
    b_near(1, 0)
    a_pair(3)
    b_near(1, 1)
    a_done(2)
    unit(2, 0)
    b_near(1, 2)
    a_near(4)
    a_done(3)
    unit(3, 0)
    b_near(1, 3)
    a_near(5)
    b_far(1, 0)
    b_far(1, 2)
    a_pair(4)
    b_far(1, 1)
    b_far(1, 3)
    b_done(1)
    unit(0, 1)
    unit(1, 1)
    a_pair(5)
    unit(2, 1)
    unit(3, 1)
    a_done(4)
    unit(4, 0)
    a_near(6)
    a_done(5)
    unit(5, 0)
    a_near(7)
    unit(4, 1)
    unit(5, 1)
    a_pair(6)
    a_pair(7)
    a_done(6)
    unit(6, 0)
    unit(6, 1)
    a_done(7)
    unit(7, 0)
    unit(7, 1)

    def sums_in():
        for at in (3, 4, 2, 5):
            for h in range(2):
                c_arrive(at, h)

    sums_in()

    def square(j, carry):
        total = [jnp.zeros((1, TILE), F32)] * 2
        for half in range(2):
            pair = []
            for h in range(2):
                value = own[half, h, j] + decoded((2 + half) * 2 + h, j) + decoded((4 + half) * 2 + h, j)
                value = value * value
                total[h] = total[h] + jnp.sum(value, axis=0, keepdims=True)
                pair.append(value)
            out_ref[half, 2 * j] = jnp.where(low, pair[0], swapped(pair[1]))
            out_ref[half, 2 * j + 1] = jnp.where(low, swapped(pair[0]), pair[1])
        t1[r, pl.ds(2 * j, 1), :] = jnp.where(low, total[0], swapped(total[1]))
        t1[r, pl.ds(2 * j + 1, 1), :] = jnp.where(low, swapped(total[0]), total[1])
        return carry

    def squares():
        lax.fori_loop(0, 8, square, 0)

    def row_exchange():
        for d in range(1, 8):
            send(t1.at[r], t1.at[r], t1_sem, (d - 1,), row_peers[d - 1])
        for d in range(1, 8):
            arrive(t1.at[(r + 8 - d) % 8], t1_sem, (d - 1,))
        t2[f] = jnp.sum(t1[...], axis=0)

    def layer_exchange():
        for d in range(1, 4):
            send(t2.at[f], t2.at[f], t2_sem, (d - 1,), fib_peers[d - 1])
        for d in range(1, 4):
            arrive(t2.at[(f + 4 - d) % 4], t2_sem, (d - 1,))
        gain_ref[...] = total_rows / (jnp.sum(t2[...], axis=0) + epsilon)

    def last_waits():
        for copy in started:
            copy.wait_send()

    squares()
    row_exchange()
    layer_exchange()
    last_waits()


def on_device(a_tiles, a_cols, a_count, b_tiles, b_cols):
    fibers = lax.axis_size("fiber")
    block_rows = b_tiles.shape[0]
    col_offset = lax.axis_index("col") * (PT // lax.axis_size("col"))
    place = a_cols // (block_rows * fibers) * block_rows + a_cols % block_rows
    place = jnp.where(jnp.arange(ASLOTS)[None, :] < a_count, place, -1)
    place = jnp.pad(place, ((0, 8), (0, SLOTS8 - ASLOTS)), constant_values=-1)
    place = jnp.pad(place, ((0, 0), (0, TILE - SLOTS8)))
    target = jnp.pad((b_cols[:, 0] - col_offset + 1)[None, :], ((8, 7), (0, TILE - block_rows)))
    meta = jnp.where(jnp.arange(16)[:, None] < 8, place, target)
    total_rows = 8 * lax.axis_size("row") * TILE
    dma = pltpu.SemaphoreType.DMA
    any_ = pl.BlockSpec(memory_space=pl.ANY)
    squares, gains = pl.pallas_call(
        functools.partial(kernel, total_rows),
        out_shape=(pltpu.VMEM((2, 16, TILE, TILE), F32), pltpu.VMEM((16, TILE), F32)),
        in_specs=[any_] * 3,
        out_specs=(pl.BlockSpec(memory_space=pltpu.VMEM),) * 2,
        scratch_shapes=[
            pltpu.VMEM((8, 8, ASLOTS, TILE, TILE), jnp.bfloat16),
            pltpu.VMEM((256, TILE, TILE), jnp.bfloat16),
            pltpu.VMEM((256, TILE, TILE), jnp.bfloat16),
            pltpu.VMEM((64, TILE, TILE), jnp.bfloat16),
            pltpu.VMEM((8, 8, TILE), jnp.int32),
            pltpu.VMEM((8, 8, TILE), jnp.int32),
            pltpu.VMEM((8, 8, TILE), jnp.int32),
            pltpu.SMEM((8, 8, TILE), jnp.int32),
            pltpu.VMEM((65, TILE, TILE), F32),
            pltpu.VMEM((12, 8, TILE, TILE), jnp.int16),
            pltpu.VMEM((12, 8, TILE), F32),
            pltpu.VMEM((12, 8, TILE, TILE), jnp.int16),
            pltpu.VMEM((12, 8, TILE), F32),
            pltpu.VMEM((2, 2, 8, TILE, TILE), F32),
            pltpu.VMEM((8, 16, TILE), F32),
            pltpu.VMEM((4, 16, TILE), F32),
            dma((5,)),
            dma((2, 7)),
            dma((2, 7)),
            dma((2, 8, 3)),
            dma((2, 8, 2)),
            dma((2, 8, 4)),
            dma((2, 2, PIECES, 3)),
            dma((2, 2, PIECES, 3)),
            dma((2, 2, PIECES)),
            dma((2, 12)),
            dma((2, 12)),
            dma((2, 7)),
            dma((2, 3)),
        ],
        compiler_params=pltpu.CompilerParams(collective_id=0, has_side_effects=True, vmem_limit_bytes=56 * 1024 * 1024),
    )(meta, a_tiles, b_tiles.reshape(block_rows, TILE, TILE))
    return squares * gains[None, :, None, :]


def solution(mesh):
    placed = (
        P("row", ("col", "fiber"), None, None),
        P("row", ("col", "fiber")),
        P("row", ("col", "fiber")),
        P(("row", "fiber"), "col", None, None),
        P(("row", "fiber"), "col"),
    )
    return jax.shard_map(
        on_device,
        mesh=mesh,
        in_specs=placed,
        out_specs=P(("row", "fiber"), "col", None, None),
        check_vma=False,
    )
```

```python
import functools

import jax
import jax.numpy as jnp
from jax import lax
from jax.experimental import pallas as pl
from jax.experimental.pallas import tpu as pltpu
from jax.sharding import PartitionSpec as P

MESH = pl.DeviceIdType.MESH
PT = 128
ASLOTS = 6
SLOTS8 = 8
TILE = 128
epsilon = 1e-06
F32 = jnp.float32
PIECES = 4
PARTS = 4
WIDE = TILE // PARTS
TOP = 32767.0


def kernel(total_rows, fibers, cols_ref, count_ref, target_ref, a_ref, b_ref, out_ref, gain_ref, pa, pb0, pb1, pb2, pb3, raw_b, ma, mn, mb, meta_v, meta_s, sums, cq_s, cs_s, cq_r, cs_r, own,
           t1, t2, loc_sem, ma_sem, mn_sem, mb_sem, ao_sem, ap_sem, af_sem, bo_sem, bk_sem, bf_sem, cq_sem, cs_sem, t1_sem, t2_sem):
    r, c, f = lax.axis_index("row"), lax.axis_index("col"), lax.axis_index("fiber")
    x, k = r // 2, r % 2
    zl, y = c // 4, c % 4
    pb = (pb0, pb1, pb2, pb3)

    def rdev(rr):
        return (rr, c, f)

    def cdev(cc):
        return (r, cc, f)

    def fdev(ff):
        return (r, c, ff)

    def rid(dx, kk):
        return ((x + dx + 4) % 4) * 2 + kk

    def cid(dy, zz):
        return zz * 4 + (y + dy + 4) % 4

    XP, XM, KP = rdev(rid(1, k)), rdev(rid(-1, k)), rdev(rid(0, 1 - k))
    YP, YM, ZP = cdev(cid(1, zl)), cdev(cid(-1, zl)), cdev(cid(0, 1 - zl))
    plus, minus, far = (f + 3 + 2 * zl) % 4, (f + 1 + 2 * zl) % 4, (f + 2) % 4
    FP, FM = fdev(plus), fdev(minus)
    row_peers = [rdev((r + d) % 8) for d in range(1, 8)]
    col_peers = [cdev((c + d) % 8) for d in range(1, 8)]
    fib_peers = [fdev((f + d) % 4) for d in range(1, 4)]

    barrier = pltpu.get_barrier_semaphore()
    for peer in row_peers + col_peers + fib_peers:
        pl.semaphore_signal(barrier, inc=1, device_id=peer, device_id_type=MESH)

    piece = 64 // PIECES
    locals_ = [
        pltpu.make_async_copy(cols_ref, ma.at[c], loc_sem.at[0]),
        pltpu.make_async_copy(target_ref, mb.at[r], loc_sem.at[1]),
        pltpu.make_async_copy(a_ref, pa.at[:, c], loc_sem.at[2]),
    ]
    for q in range(PIECES):
        part = pl.ds(q * piece, piece)
        locals_.append(pltpu.make_async_copy(b_ref.at[part], raw_b.at[part], loc_sem.at[4 + q]))
    locals_.append(pltpu.make_async_copy(count_ref, mn.at[c], loc_sem.at[4 + PIECES]))
    for copy in locals_:
        copy.start()
    for q in range(3 * PARTS):
        sums[q, 0] = jnp.zeros((WIDE, TILE), F32)

    sum_set = (0, 0, 0, 0, 1, 2, 0, 1)
    started = []

    def send(src, dst, sem, at, device):
        copy = pltpu.make_async_remote_copy(
            src_ref=src, dst_ref=dst, send_sem=sem.at[(0,) + at], recv_sem=sem.at[(1,) + at], device_id=device, device_id_type=MESH
        )
        copy.start()
        started.append(copy)

    def arrive(dst, sem, at):
        pltpu.make_async_remote_copy(
            src_ref=dst, dst_ref=dst, send_sem=sem.at[(0,) + at], recv_sem=sem.at[(1,) + at], device_id=KP, device_id_type=MESH
        ).wait_recv()

    def flip_b(q):
        def one_tile(n, carry):
            tile = raw_b[n].T
            for h in range(PARTS):
                pb[h][r * 64 + n] = tile[h * WIDE : (h + 1) * WIDE]
            return carry

        locals_[3 + q].wait()
        lax.fori_loop(q * piece, (q + 1) * piece, one_tile, 0)

    def b_at(h, block, q):
        return pb[h].at[pl.ds(block * 64 + q * piece, piece)]

    def b_own(h, q):
        part = b_at(h, r, q)
        send(part, part, bo_sem, (h, q, 1), XP)
        send(part, part, bo_sem, (h, q, 2), XM)
        send(part, part, bo_sem, (h, q, 0), KP)

    def b_all(h):
        for q in range(PIECES):
            b_own(h, q)

    def b_near(h, q):
        part = b_at(h, rid(-1, k), q)
        arrive(part, bo_sem, (h, q, 1))
        if q < PIECES // 2:
            send(part, part, bf_sem, (h, q), XP)
        send(part, part, bk_sem, (h, q, 0), KP)
        part = b_at(h, rid(1, k), q)
        arrive(part, bo_sem, (h, q, 2))
        if q >= PIECES // 2:
            send(part, part, bf_sem, (h, q), XM)
        send(part, part, bk_sem, (h, q, 1), KP)

    def b_far(h, q):
        for at in (q, q + PIECES // 2):
            part = b_at(h, rid(2, k), at)
            arrive(part, bf_sem, (h, at))
            send(part, part, bk_sem, (h, at, 2), KP)

    def b_done(h):
        for q in range(PIECES):
            arrive(b_at(h, rid(0, 1 - k), q), bo_sem, (h, q, 0))
            arrive(b_at(h, rid(-1, 1 - k), q), bk_sem, (h, q, 0))
            arrive(b_at(h, rid(1, 1 - k), q), bk_sem, (h, q, 1))
            arrive(b_at(h, rid(2, 1 - k), q), bk_sem, (h, q, 2))

    rows = [far * 2, far * 2 + 1, plus * 2 + 1, minus * 2, plus * 2, minus * 2 + 1, f * 2, f * 2 + 1]
    pair_rows = [far * 2, far * 2 + 1, minus * 2 + 1, plus * 2, minus * 2, plus * 2 + 1, f * 2, f * 2 + 1]

    def a_own(n, ways):
        for way, device in enumerate((ZP, YP, YM)):
            row = rows[n] if way else pair_rows[n]
            if way in ways:
                send(a_ref.at[row], pa.at[row, c], ao_sem, (n, way), device)

    def a_half(n, block, half, way, device):
        part = pa.at[rows[n], block, pl.ds(half * 3, 3)]
        send(part, part, af_sem, (n, way), device)

    def a_near(n):
        row = rows[n]
        block = cid(0, 1 - zl)
        arrive(pa.at[row, block], ao_sem, (n, 0))
        for way, device in enumerate((YP, YM)):
            send(pa.at[row, block], pa.at[row, block], ap_sem, (n, way), device)
        arrive(pa.at[row, cid(-1, zl)], ao_sem, (n, 1))
        a_half(n, cid(-1, zl), 0, 0, YP)
        arrive(pa.at[row, cid(1, zl)], ao_sem, (n, 2))
        a_half(n, cid(1, zl), 1, 1, YM)
        if n < 2:
            for later in range(3 + n * 3, min(6 + n * 3, 8)):
                a_own(later, (0,))

    def a_pair(n):
        row = rows[n]
        arrive(pa.at[row, cid(-1, 1 - zl)], ap_sem, (n, 0))
        a_half(n, cid(-1, 1 - zl), 0, 2, YP)
        arrive(pa.at[row, cid(1, 1 - zl)], ap_sem, (n, 1))
        a_half(n, cid(1, 1 - zl), 1, 3, YM)
        if n + 2 < 8:
            a_own(n + 2, (1, 2))

    def a_done(n):
        row = rows[n]
        for way, (zz, half) in enumerate(((zl, 0), (zl, 1), (1 - zl, 0), (1 - zl, 1))):
            arrive(pa.at[row, cid(2, zz), pl.ds(half * 3, 3)], af_sem, (n, way))

    def block_of(o):
        return ((zl + o) % 2) * 4 + (y + o // 2 + 3) % 4

    def index_tables():
        for d in range(1, 8):
            arrive(ma.at[(c + 8 - d) % 8], ma_sem, (d - 1,))
            arrive(mn.at[(c + 8 - d) % 8], mn_sem, (d - 1,))
            arrive(mb.at[(r + 8 - d) % 8], mb_sem, (d - 1,))
        lane = lax.broadcasted_iota(jnp.int32, (64, TILE), 1)
        slot = lax.broadcasted_iota(jnp.int32, (64, TILE), 0)
        kept = slot - (SLOTS8 - ASLOTS) * (slot // SLOTS8) + 1
        lane6 = lax.broadcasted_iota(jnp.int32, (8, ASLOTS), 1)
        slot6 = lax.broadcasted_iota(jnp.int32, (8, ASLOTS), 0)
        lane_n = lax.broadcasted_iota(jnp.int32, (1, 8), 1)

        def one_row(i, carry):
            place = []
            for o in range(8):
                block = block_of(o)
                part = jnp.broadcast_to(ma[block, pl.ds(i, 1), :], (8, ASLOTS))
                part = jnp.sum(jnp.where(slot6 == lane6, part, 0), axis=1, keepdims=True)
                live = jnp.sum(jnp.where(lane_n == i, mn[block], 0), axis=1, keepdims=True)
                part = jnp.broadcast_to(part, (8, TILE))
                part = part // (64 * fibers) * 64 + part % 64
                live = slot[:8] < jnp.broadcast_to(live, (8, TILE))
                place.append(jnp.where(live, part, -1))
            place = jnp.concatenate(place, axis=0)
            target = jnp.zeros((64, 64), jnp.int32)
            for q in range(8):
                hit = place[:, :64] == lane[:, :64] + q * 64
                target = target + jnp.where(hit, mb[q] - c * 16 + 1, 0)
            target = jnp.sum(target, axis=1, keepdims=True)
            target = jnp.broadcast_to(target, (64, TILE))
            here = slot == lane
            target_l = jnp.sum(jnp.where(here, target, 0), axis=0, keepdims=True)
            place_l = jnp.sum(jnp.where(here, jnp.maximum(place, 0), 0), axis=0, keepdims=True)
            same = (target == target_l) & (slot < lane) & (target > 0)
            prev = jnp.max(jnp.where(same, kept, 0), axis=0, keepdims=True)
            last = jnp.max(jnp.where(target == lane + 1, kept, 0), axis=0, keepdims=True)
            meta_v[i, 0:1, :] = place_l
            meta_v[i, 1:2, :] = prev
            meta_v[i, 2:3, :] = last
            return carry

        lax.fori_loop(0, 8, one_row, 0)
        copy = pltpu.make_async_copy(meta_v, meta_s, loc_sem.at[3])
        copy.start()
        copy.wait()
        locals_[2].wait()

    def products(n, parts, first=0, stop=8):
        row = rows[n]
        into = PARTS * sum_set[n]

        def one_block(o, carry):
            block = block_of(o)
            for e in range(ASLOTS):
                t = o * SLOTS8 + e
                place, prev = meta_s[row, 0, t], meta_s[row, 1, t]
                left = jnp.concatenate([pb[h][place] for h in parts], axis=0)
                product = lax.dot_general(left, pa[row, block, e], (((1,), (1,)), ((), ())), preferred_element_type=F32)
                for n_h, h in enumerate(parts):
                    sums[into + h, 1 + o * ASLOTS + e] = product[n_h * WIDE : (n_h + 1) * WIDE] + sums[into + h, prev]
            return carry

        lax.fori_loop(first, stop, one_block, 0)

    wide_lane = lax.broadcasted_iota(jnp.int32, (WIDE, TILE), 1)
    wide_slot = lax.broadcasted_iota(jnp.int32, (WIDE, TILE), 0)

    def to_lanes(column, i):
        return jnp.sum(jnp.where(wide_lane == wide_slot + i * WIDE, column, 0.0), axis=0, keepdims=True)

    def to_column(row, i):
        return jnp.sum(jnp.where(wide_lane == wide_slot + i * WIDE, row, 0.0), axis=1, keepdims=True)

    def decoded(at, g, i):
        return cq_r[at, g * 4 + i].astype(jnp.int32).astype(F32) * to_column(cs_r[at, pl.ds(g, 1), :], i)

    def emit(n, h, at, device, add=None):
        row = rows[n]
        at = at * PARTS + h

        def four_tiles(g, carry):
            scales = jnp.zeros((1, TILE), F32)
            for i in range(4):
                value = sums[PARTS * sum_set[n] + h, meta_s[row, 2, g * 4 + i]]
                if add is not None:
                    value = value + decoded(add * PARTS + h, g, i)
                top = jnp.max(jnp.abs(value), axis=1, keepdims=True)
                gain = jnp.where(top > 1e-30, TOP / jnp.maximum(top, 1e-30), 0.0)
                cq_s[at, g * 4 + i] = jnp.floor(value * gain + 0.5).astype(jnp.int32).astype(jnp.int16)
                scales = scales + to_lanes(top * (1.0 / TOP), i)
            cs_s[at, pl.ds(g, 1), :] = scales
            return carry

        lax.fori_loop(0, 4, four_tiles, 0)
        send(cs_s.at[at], cs_r.at[at], cs_sem, (at,), device)
        send(cq_s.at[at], cq_r.at[at], cq_sem, (at,), device)

    def c_arrive(at, h):
        at = at * PARTS + h
        arrive(cs_r.at[at], cs_sem, (at,))
        arrive(cq_r.at[at], cq_sem, (at,))

    def gather(h):
        for at in (3, 4, 2, 5):
            c_arrive(at, h)

        def four_tiles(g, carry):
            for i in range(4):
                for half in range(2):
                    own[half, h, g * 4 + i] = decoded((2 + half) * PARTS + h, g, i) + decoded((4 + half) * PARTS + h, g, i)
            return carry

        lax.fori_loop(0, 4, four_tiles, 0)

    def finish(n, h):
        row = rows[n]

        def four_tiles(g, carry):
            for i in range(4):
                j = g * 4 + i
                value = own[n - 6, h, j] + sums[PARTS * sum_set[n] + h, meta_s[row, 2, j]]
                value = value * value
                own[n - 6, h, j] = value
                total = to_lanes(jnp.sum(value, axis=1, keepdims=True), h)
                if (n, h) != (6, 0):
                    total = total + t1[r, pl.ds(j, 1), :]
                t1[r, pl.ds(j, 1), :] = total
            return carry

        lax.fori_loop(0, 4, four_tiles, 0)

    slots = ((0, FP, None), (1, FM, None), (3, FP, None), (4, FM, None), (2, FP, 0), (5, FM, 1))

    def give(n, h):
        at, device, add = slots[n]
        if add is not None:
            c_arrive(add, h)
        emit(n, h, at, device, add)

    def unit(n, *parts):
        products(n, parts)
        for h in parts:
            give(n, h)

    every = tuple(range(PARTS))

    def start():
        flip_b(0)
        pl.semaphore_wait(barrier, len(row_peers) + len(col_peers) + len(fib_peers))
        a_own(0, (0, 1, 2))
        b_own(0, 0)
        for n in (0, 1, -1):
            locals_[n].wait()
        for d in range(1, 8):
            send(ma.at[c], ma.at[c], ma_sem, (d - 1,), col_peers[d - 1])
            send(mn.at[c], mn.at[c], mn_sem, (d - 1,), col_peers[d - 1])
            send(mb.at[r], mb.at[r], mb_sem, (d - 1,), row_peers[d - 1])

    def start_b():
        flip_b(1)
        b_own(0, 1)
        a_own(1, (0, 1, 2))
        flip_b(2)
        b_own(0, 2)
        a_own(2, (0,))
        flip_b(3)
        b_own(0, 3)

    def last_waits():
        for copy in started:
            copy.wait_send()
        started.clear()

    start()
    start_b()
    b_near(0, 0)
    a_near(0)
    b_near(0, 1)
    b_near(0, 2)
    b_near(0, 3)
    b_all(1)
    a_pair(0)
    a_near(1)
    index_tables()
    b_far(0, 0)
    b_far(0, 1)
    b_done(0)
    a_done(0)
    unit(0, 0)
    b_near(1, 0)
    b_near(1, 1)
    a_pair(1)
    a_near(2)
    b_near(1, 2)
    b_near(1, 3)
    b_all(2)
    a_done(1)
    unit(1, 0)
    b_far(1, 0)
    b_far(1, 1)
    b_done(1)
    a_pair(2)
    a_near(3)
    unit(0, 1)
    b_near(2, 0)
    unit(1, 1)
    b_near(2, 1)
    b_near(2, 2)
    a_done(2)
    unit(2, 0, 1)
    b_near(2, 3)
    b_all(3)
    b_far(2, 0)
    a_pair(3)
    a_near(4)
    b_far(2, 1)
    b_done(2)
    unit(1, 2)
    unit(0, 2)
    b_near(3, 0)
    b_near(3, 1)
    a_done(3)
    unit(3, 0, 1)
    a_pair(4)
    a_near(5)
    b_near(3, 2)
    unit(2, 2)
    b_near(3, 3)
    unit(3, 2)
    a_done(4)
    products(4, (0, 1, 2))
    give(4, 0)
    b_far(3, 0)
    b_far(3, 1)
    b_done(3)
    unit(1, 3)
    unit(0, 3)
    a_pair(5)
    a_near(6)
    give(4, 1)
    unit(3, 3)
    a_done(5)
    products(5, every)
    give(5, 0)
    give(4, 2)
    give(5, 1)
    unit(2, 3)
    a_pair(6)
    a_near(7)
    give(5, 2)
    products(4, (3,))
    give(4, 3)
    give(5, 3)
    products(6, every, 0, 6)
    a_pair(7)
    a_done(6)
    products(6, every, 6, 8)
    products(7, every, 0, 6)
    gather(0)
    finish(6, 0)
    a_done(7)
    products(7, every, 6, 8)
    finish(7, 0)
    gather(1)
    finish(6, 1)
    finish(7, 1)
    gather(2)
    finish(6, 2)
    finish(7, 2)
    last_waits()
    gather(3)
    finish(6, 3)
    finish(7, 3)

    def flip_out(j, carry):
        for half in range(2):
            out_ref[half, j] = jnp.concatenate([own[half, h, j] for h in range(PARTS)], axis=0).T
        return carry

    def row_exchange():
        for d in range(1, 8):
            send(t1.at[r], t1.at[r], t1_sem, (d - 1,), row_peers[d - 1])
        for d in range(1, 8):
            arrive(t1.at[(r + 8 - d) % 8], t1_sem, (d - 1,))
        t2[f] = jnp.sum(t1[...], axis=0)

    def layer_exchange():
        for d in range(1, 4):
            send(t2.at[f], t2.at[f], t2_sem, (d - 1,), fib_peers[d - 1])
        lax.fori_loop(0, 16, flip_out, 0)
        for d in range(1, 4):
            arrive(t2.at[(f + 4 - d) % 4], t2_sem, (d - 1,))
        gain_ref[...] = total_rows / (jnp.sum(t2[...], axis=0) + epsilon)

    row_exchange()
    layer_exchange()
    last_waits()


def on_device(a_tiles, a_cols, a_count, b_tiles, b_cols):
    block_rows = b_tiles.shape[0]
    total_rows = 8 * lax.axis_size("row") * TILE
    dma = pltpu.SemaphoreType.DMA
    any_ = pl.BlockSpec(memory_space=pl.ANY)
    squares, gains = pl.pallas_call(
        functools.partial(kernel, total_rows, lax.axis_size("fiber")),
        out_shape=(pltpu.VMEM((2, 16, TILE, TILE), F32), pltpu.VMEM((16, TILE), F32)),
        in_specs=[any_] * 5,
        out_specs=(pl.BlockSpec(memory_space=pltpu.VMEM),) * 2,
        scratch_shapes=[
            pltpu.VMEM((8, 8, ASLOTS, TILE, TILE), jnp.bfloat16),
            *[pltpu.VMEM((512, WIDE, TILE), jnp.bfloat16)] * PARTS,
            pltpu.VMEM((64, TILE, TILE), jnp.bfloat16),
            pltpu.VMEM((8, 8, ASLOTS), jnp.int32),
            pltpu.VMEM((8, 1, 8), jnp.int32),
            pltpu.VMEM((8, 1, 64), jnp.int32),
            pltpu.VMEM((8, 8, TILE), jnp.int32),
            pltpu.SMEM((8, 8, TILE), jnp.int32),
            pltpu.VMEM((3 * PARTS, 1 + 8 * ASLOTS, WIDE, TILE), F32),
            pltpu.VMEM((6 * PARTS, 16, WIDE, TILE), jnp.int16),
            pltpu.VMEM((6 * PARTS, 4, TILE), F32),
            pltpu.VMEM((6 * PARTS, 16, WIDE, TILE), jnp.int16),
            pltpu.VMEM((6 * PARTS, 4, TILE), F32),
            pltpu.VMEM((2, PARTS, 16, WIDE, TILE), F32),
            pltpu.VMEM((8, 16, TILE), F32),
            pltpu.VMEM((4, 16, TILE), F32),
            dma((5 + PIECES,)),
            dma((2, 7)),
            dma((2, 7)),
            dma((2, 7)),
            dma((2, 8, 3)),
            dma((2, 8, 2)),
            dma((2, 8, 4)),
            dma((2, PARTS, PIECES, 3)),
            dma((2, PARTS, PIECES, 3)),
            dma((2, PARTS, PIECES)),
            dma((2, 6 * PARTS)),
            dma((2, 6 * PARTS)),
            dma((2, 7)),
            dma((2, 3)),
        ],
        compiler_params=pltpu.CompilerParams(collective_id=0, has_side_effects=True, vmem_limit_bytes=56 * 1024 * 1024),
    )(a_cols, a_count.reshape(1, 8), b_cols.reshape(1, block_rows), a_tiles, b_tiles.reshape(block_rows, TILE, TILE))
    return squares * gains[None, :, None, :]


def solution(mesh):
    placed = (
        P("row", ("col", "fiber"), None, None),
        P("row", ("col", "fiber")),
        P("row", ("col", "fiber")),
        P(("row", "fiber"), "col", None, None),
        P(("row", "fiber"), "col"),
    )
    return jax.shard_map(
        on_device,
        mesh=mesh,
        in_specs=placed,
        out_specs=P(("row", "fiber"), "col", None, None),
        check_vma=False,
    )
```

```python
import functools

import jax
import jax.numpy as jnp
from jax import lax
from jax.experimental import pallas as pl
from jax.experimental.pallas import tpu as pltpu
from jax.sharding import PartitionSpec as P

MESH = pl.DeviceIdType.MESH
PT = 128
ASLOTS = 6
SLOTS8 = 8
TILE = 128
epsilon = 1e-06
F32 = jnp.float32
PIECES = 4
PARTS = 4
WIDE = TILE // PARTS
TOP = 32767.0


def kernel(total_rows, fibers, cols_ref, count_ref, target_ref, a_ref, b_ref, result_ref, gain_ref, pa, pb0, pb1, pb2, pb3, raw_b, ma, mn, mb, meta_v, meta_s, sums, cq_s, cs_s, cq_r, cs_r, own, out_ref,
           t1, t2, loc_sem, out_sem, m_sem, ao_sem, ap_sem, af_sem, bn_sem, bf_sem, kp_sem, far_sem, sum_sem, t_sem):
    r, c, f = lax.axis_index("row"), lax.axis_index("col"), lax.axis_index("fiber")
    x, k = r // 2, r % 2
    zl, y = c // 4, c % 4
    pb = (pb0, pb1, pb2, pb3)

    def rdev(rr):
        return (rr, c, f)

    def cdev(cc):
        return (r, cc, f)

    def fdev(ff):
        return (r, c, ff)

    def rid(dx, kk):
        return ((x + dx + 4) % 4) * 2 + kk

    def cid(dy, zz):
        return zz * 4 + (y + dy + 4) % 4

    XP, XM, KP = rdev(rid(1, k)), rdev(rid(-1, k)), rdev(rid(0, 1 - k))
    YP, YM, ZP = cdev(cid(1, zl)), cdev(cid(-1, zl)), cdev(cid(0, 1 - zl))
    plus, minus, far = (f + 3 + 2 * zl) % 4, (f + 1 + 2 * zl) % 4, (f + 2) % 4
    FP, FM = fdev(plus), fdev(minus)
    row_peers = [rdev((r + d) % 8) for d in range(1, 8)]
    col_peers = [cdev((c + d) % 8) for d in range(1, 8)]
    fib_peers = [fdev((f + d) % 4) for d in range(1, 4)]

    barrier = pltpu.get_barrier_semaphore()
    for peer in row_peers + col_peers + fib_peers:
        pl.semaphore_signal(barrier, inc=1, device_id=peer, device_id_type=MESH)

    piece = 64 // PIECES
    locals_ = [
        pltpu.make_async_copy(cols_ref, ma.at[c], loc_sem.at[0]),
        pltpu.make_async_copy(target_ref, mb.at[r], loc_sem.at[1]),
        pltpu.make_async_copy(a_ref, pa.at[:, c], loc_sem.at[2]),
    ]
    for q in range(PIECES):
        part = pl.ds(q * piece, piece)
        locals_.append(pltpu.make_async_copy(b_ref.at[part], raw_b.at[part], loc_sem.at[4 + q]))
    locals_.append(pltpu.make_async_copy(count_ref, mn.at[c], loc_sem.at[4 + PIECES]))
    for copy in locals_:
        copy.start()
    for q in range(3 * PARTS):
        sums[q, 0] = jnp.zeros((WIDE, TILE), F32)

    sum_set = (0, 0, 0, 0, 1, 2, 0, 1)

    def send(src, dst, out, into, device):
        pltpu.make_async_remote_copy(
            src_ref=src, dst_ref=dst, send_sem=out_sem.at[out], recv_sem=into, device_id=device, device_id_type=MESH
        ).start()

    def arrive(dst, into):
        pltpu.make_async_remote_copy(
            src_ref=dst, dst_ref=dst, send_sem=out_sem.at[0], recv_sem=into, device_id=KP, device_id_type=MESH
        ).wait_recv()

    def left(src, out):
        pltpu.make_async_remote_copy(
            src_ref=src, dst_ref=src, send_sem=out_sem.at[out], recv_sem=m_sem.at[0], device_id=KP, device_id_type=MESH
        ).wait_send()

    AO, AP, AF, CQ, CS, MA, MN, MB, T1, T2, BO, BK, BF = 0, 1, 2, 3, 4, 5, 6, 7, 8, 9, 10, 14, 18

    def flip_b(q):
        def one_tile(n, carry):
            tile = raw_b[n].T
            for h in range(PARTS):
                pb[h][r * 64 + n] = tile[h * WIDE : (h + 1) * WIDE]
            return carry

        locals_[3 + q].wait()
        lax.fori_loop(q * piece, (q + 1) * piece, one_tile, 0)

    def b_at(h, block, q):
        return pb[h].at[pl.ds(block * 64 + q * piece, piece)]

    def b_own(h, q):
        part = b_at(h, r, q)
        send(part, part, BO + h, bn_sem.at[h, q, 0], XP)
        send(part, part, BO + h, bn_sem.at[h, q, 1], XM)
        send(part, part, BO + h, kp_sem.at[h], KP)

    def b_all(h):
        for q in range(PIECES):
            b_own(h, q)

    def b_near(h, q):
        part = b_at(h, rid(-1, k), q)
        arrive(part, bn_sem.at[h, q, 0])
        if q < PIECES // 2:
            send(part, part, BF + h, bf_sem.at[h, q], XP)
        send(part, part, BK + h, kp_sem.at[h], KP)
        part = b_at(h, rid(1, k), q)
        arrive(part, bn_sem.at[h, q, 1])
        if q >= PIECES // 2:
            send(part, part, BF + h, bf_sem.at[h, q], XM)
        send(part, part, BK + h, kp_sem.at[h], KP)

    def b_far(h, q):
        for at in (q, q + PIECES // 2):
            part = b_at(h, rid(2, k), at)
            arrive(part, bf_sem.at[h, at])
            send(part, part, BK + h, kp_sem.at[h], KP)

    def b_done(h):
        arrive(pb[h].at[pl.ds(0, 256)], kp_sem.at[h])

    rows = [far * 2, far * 2 + 1, plus * 2 + 1, minus * 2, plus * 2, minus * 2 + 1, f * 2, f * 2 + 1]
    pair_rows = [far * 2, far * 2 + 1, minus * 2 + 1, plus * 2, minus * 2, plus * 2 + 1, f * 2, f * 2 + 1]

    def a_own(n, ways):
        for way, device in enumerate((ZP, YP, YM)):
            row = rows[n] if way else pair_rows[n]
            if way in ways:
                send(a_ref.at[row], pa.at[row, c], AO, ao_sem.at[n, way], device)

    def a_half(n, block, half, device):
        part = pa.at[rows[n], block, pl.ds(half * 3, 3)]
        send(part, part, AF, af_sem.at[n], device)

    def a_near(n):
        row = rows[n]
        block = cid(0, 1 - zl)
        arrive(pa.at[row, block], ao_sem.at[n, 0])
        for way, device in enumerate((YP, YM)):
            send(pa.at[row, block], pa.at[row, block], AP, ap_sem.at[n, way], device)
        arrive(pa.at[row, cid(-1, zl)], ao_sem.at[n, 1])
        a_half(n, cid(-1, zl), 0, YP)
        arrive(pa.at[row, cid(1, zl)], ao_sem.at[n, 2])
        a_half(n, cid(1, zl), 1, YM)
        if n < 2:
            for later in range(3 + n * 3, min(6 + n * 3, 8)):
                a_own(later, (0,))

    def a_pair(n):
        row = rows[n]
        arrive(pa.at[row, cid(-1, 1 - zl)], ap_sem.at[n, 0])
        a_half(n, cid(-1, 1 - zl), 0, YP)
        arrive(pa.at[row, cid(1, 1 - zl)], ap_sem.at[n, 1])
        a_half(n, cid(1, 1 - zl), 1, YM)
        if n + 2 < 8:
            a_own(n + 2, (1, 2))

    def a_done(n):
        arrive(pa.at[rows[n], pl.ds(0, 2)], af_sem.at[n])

    def block_of(o):
        return ((zl + o) % 2) * 4 + (y + o // 2 + 3) % 4

    def index_tables():
        for n, ref in enumerate((ma, mn, mb)):
            arrive(ref.at[pl.ds(0, 7)], m_sem.at[n])
        lane = lax.broadcasted_iota(jnp.int32, (64, TILE), 1)
        slot = lax.broadcasted_iota(jnp.int32, (64, TILE), 0)
        kept = slot - (SLOTS8 - ASLOTS) * (slot // SLOTS8) + 1
        lane6 = lax.broadcasted_iota(jnp.int32, (8, ASLOTS), 1)
        slot6 = lax.broadcasted_iota(jnp.int32, (8, ASLOTS), 0)
        lane_n = lax.broadcasted_iota(jnp.int32, (1, 8), 1)

        def one_row(i, carry):
            place = []
            for o in range(8):
                block = block_of(o)
                part = jnp.broadcast_to(ma[block, pl.ds(i, 1), :], (8, ASLOTS))
                part = jnp.sum(jnp.where(slot6 == lane6, part, 0), axis=1, keepdims=True)
                live = jnp.sum(jnp.where(lane_n == i, mn[block], 0), axis=1, keepdims=True)
                part = jnp.broadcast_to(part, (8, TILE))
                part = part // (64 * fibers) * 64 + part % 64
                live = slot[:8] < jnp.broadcast_to(live, (8, TILE))
                place.append(jnp.where(live, part, -1))
            place = jnp.concatenate(place, axis=0)
            target = jnp.zeros((64, 64), jnp.int32)
            for q in range(8):
                hit = place[:, :64] == lane[:, :64] + q * 64
                target = target + jnp.where(hit, mb[q] - c * 16 + 1, 0)
            target = jnp.sum(target, axis=1, keepdims=True)
            target = jnp.broadcast_to(target, (64, TILE))
            here = slot == lane
            target_l = jnp.sum(jnp.where(here, target, 0), axis=0, keepdims=True)
            place_l = jnp.sum(jnp.where(here, jnp.maximum(place, 0), 0), axis=0, keepdims=True)
            same = (target == target_l) & (slot < lane) & (target > 0)
            prev = jnp.max(jnp.where(same, kept, 0), axis=0, keepdims=True)
            last = jnp.max(jnp.where(target == lane + 1, kept, 0), axis=0, keepdims=True)
            meta_v[i, 0:1, :] = place_l
            meta_v[i, 1:2, :] = prev
            meta_v[i, 2:3, :] = last
            return carry

        lax.fori_loop(0, 8, one_row, 0)
        copy = pltpu.make_async_copy(meta_v, meta_s, loc_sem.at[3])
        copy.start()
        copy.wait()
        locals_[2].wait()

    def products(n, parts, first=0, stop=8):
        row = rows[n]
        into = PARTS * sum_set[n]

        def one_block(o, carry):
            block = block_of(o)
            for e in range(ASLOTS):
                t = o * SLOTS8 + e
                place, prev = meta_s[row, 0, t], meta_s[row, 1, t]
                left = jnp.concatenate([pb[h][place] for h in parts], axis=0)
                product = lax.dot_general(left, pa[row, block, e], (((1,), (1,)), ((), ())), preferred_element_type=F32)
                for n_h, h in enumerate(parts):
                    sums[into + h, 1 + o * ASLOTS + e] = product[n_h * WIDE : (n_h + 1) * WIDE] + sums[into + h, prev]
            return carry

        lax.fori_loop(first, stop, one_block, 0, unroll=4 if stop - first == 8 else 2)

    wide_lane = lax.broadcasted_iota(jnp.int32, (WIDE, TILE), 1)
    wide_slot = lax.broadcasted_iota(jnp.int32, (WIDE, TILE), 0)

    def to_lanes(column, i):
        return jnp.sum(jnp.where(wide_lane == wide_slot + i * WIDE, column, 0.0), axis=0, keepdims=True)

    def to_column(row, i):
        return jnp.sum(jnp.where(wide_lane == wide_slot + i * WIDE, row, 0.0), axis=1, keepdims=True)

    def decoded(at, g, i):
        return cq_r[at, g * 4 + i].astype(jnp.int32).astype(F32) * to_column(cs_r[at, pl.ds(g, 1), :], i)

    def emit(n, h, at, device, add=None):
        row = rows[n]
        slot = at
        at = h * 6 + at

        def four_tiles(g, carry):
            scales = jnp.zeros((1, TILE), F32)
            for i in range(4):
                value = sums[PARTS * sum_set[n] + h, meta_s[row, 2, g * 4 + i]]
                if add is not None:
                    value = value + decoded(h * 6 + add, g, i)
                top = jnp.max(jnp.abs(value), axis=1, keepdims=True)
                gain = jnp.where(top > 1e-30, TOP / jnp.maximum(top, 1e-30), 0.0)
                cq_s[at, g * 4 + i] = jnp.floor(value * gain + 0.5).astype(jnp.int32).astype(jnp.int16)
                scales = scales + to_lanes(top * (1.0 / TOP), i)
            cs_s[at, pl.ds(g, 1), :] = scales
            return carry

        lax.fori_loop(0, 4, four_tiles, 0)
        into = [far_sem.at[n, slot, h] if slot < 2 else sum_sem.at[n, h] for n in range(2)]
        send(cs_s.at[at], cs_r.at[at], CS, into[0], device)
        send(cq_s.at[at], cq_r.at[at], CQ, into[1], device)

    def c_arrive(at, h):
        arrive(cs_r.at[h * 6 + at], far_sem.at[0, at, h])
        arrive(cq_r.at[h * 6 + at], far_sem.at[1, at, h])

    def gather(h):
        arrive(cs_r.at[pl.ds(h * 6 + 2, 4)], sum_sem.at[0, h])
        arrive(cq_r.at[pl.ds(h * 6 + 2, 4)], sum_sem.at[1, h])

        def four_tiles(g, carry):
            for i in range(4):
                for half in range(2):
                    own[half, h, g * 4 + i] = decoded(h * 6 + 2 + half, g, i) + decoded(h * 6 + 4 + half, g, i)
            return carry

        lax.fori_loop(0, 4, four_tiles, 0)

    def finish(n, h):
        row = rows[n]

        def four_tiles(g, carry):
            for i in range(4):
                j = g * 4 + i
                value = own[n - 6, h, j] + sums[PARTS * sum_set[n] + h, meta_s[row, 2, j]]
                value = value * value
                own[n - 6, h, j] = value
                total = to_lanes(jnp.sum(value, axis=1, keepdims=True), h)
                if (n, h) != (6, 0):
                    total = total + t1[r, pl.ds(j, 1), :]
                t1[r, pl.ds(j, 1), :] = total
            return carry

        lax.fori_loop(0, 4, four_tiles, 0)

    slots = ((0, FP, None), (1, FM, None), (3, FP, None), (4, FM, None), (2, FP, 0), (5, FM, 1))

    def give(n, h):
        at, device, add = slots[n]
        if add is not None:
            c_arrive(add, h)
        emit(n, h, at, device, add)

    def unit(n, *parts):
        products(n, parts)
        for h in parts:
            give(n, h)

    every = tuple(range(PARTS))

    def start():
        flip_b(0)
        pl.semaphore_wait(barrier, len(row_peers) + len(col_peers) + len(fib_peers))
        a_own(0, (0, 1, 2))
        b_own(0, 0)
        for n in (0, 1, -1):
            locals_[n].wait()
        for d in range(1, 8):
            send(ma.at[c], ma.at[c], MA, m_sem.at[0], col_peers[d - 1])
            send(mn.at[c], mn.at[c], MN, m_sem.at[1], col_peers[d - 1])
            send(mb.at[r], mb.at[r], MB, m_sem.at[2], row_peers[d - 1])

    def start_b():
        flip_b(1)
        b_own(0, 1)
        a_own(1, (0, 1, 2))
        flip_b(2)
        b_own(0, 2)
        a_own(2, (0,))
        flip_b(3)
        b_own(0, 3)

    def last_waits():
        left(pa.at[pl.ds(0, 3)], AO)
        left(pa.at[pl.ds(0, 2)], AP)
        left(pa.at[pl.ds(0, 2)], AF)
        left(cq_s, CQ)
        left(cs_s, CS)
        left(ma.at[pl.ds(0, 7)], MA)
        left(mn.at[pl.ds(0, 7)], MN)
        left(mb.at[pl.ds(0, 7)], MB)
        for h in range(PARTS):
            left(pb[h].at[pl.ds(0, 192)], BO + h)
            left(pb[h].at[pl.ds(0, 192)], BK + h)
            left(pb[h].at[pl.ds(0, 64)], BF + h)

    start()
    start_b()
    b_near(0, 0)
    a_near(0)
    b_near(0, 1)
    index_tables()
    b_near(0, 2)
    b_near(0, 3)
    b_all(1)
    a_pair(0)
    a_near(1)
    b_far(0, 0)
    b_far(0, 1)
    b_done(0)
    a_done(0)
    unit(0, 0)
    b_near(1, 0)
    b_near(1, 1)
    b_near(1, 2)
    a_pair(1)
    a_near(2)
    b_near(1, 3)
    b_all(2)
    a_done(1)
    unit(1, 0)
    b_far(1, 0)
    b_far(1, 1)
    b_done(1)
    unit(0, 1)
    b_near(2, 0)
    a_pair(2)
    a_near(3)
    unit(1, 1)
    b_near(2, 1)
    b_near(2, 2)
    a_done(2)
    unit(2, 0, 1)
    b_near(2, 3)
    b_all(3)
    b_far(2, 0)
    a_pair(3)
    a_near(4)
    b_far(2, 1)
    b_done(2)
    unit(1, 2)
    unit(0, 2)
    b_near(3, 0)
    b_near(3, 1)
    a_done(3)
    unit(3, 0, 1)
    b_near(3, 2)
    b_near(3, 3)
    a_pair(4)
    a_near(5)
    unit(2, 2)
    unit(3, 2)
    b_far(3, 0)
    b_far(3, 1)
    a_done(4)
    products(4, (0, 1, 2))
    b_done(3)
    unit(1, 3)
    unit(0, 3)
    give(4, 0)
    give(4, 1)
    a_pair(5)
    a_near(6)
    give(4, 2)
    unit(3, 3)
    unit(2, 3)
    products(4, (3,))
    a_done(5)
    products(5, every)
    give(5, 0)
    give(5, 1)
    give(5, 2)
    give(4, 3)
    a_pair(6)
    a_near(7)
    products(6, every, 0, 6)
    give(5, 3)
    a_done(6)
    products(6, every, 6, 8)
    a_pair(7)
    products(7, every, 0, 6)
    gather(0)
    finish(6, 0)
    gather(1)
    finish(6, 1)
    a_done(7)
    products(7, every, 6, 8)
    finish(7, 0)
    finish(7, 1)
    gather(2)
    finish(6, 2)
    finish(7, 2)
    last_waits()
    gather(3)
    finish(6, 3)
    finish(7, 3)

    results = [pltpu.make_async_copy(out_ref.at[half], result_ref.at[half], loc_sem.at[5 + PIECES + half]) for half in range(2)]

    def flip_out(half):
        def one_tile(j, carry):
            out_ref[half, j] = jnp.concatenate([own[half, h, j] for h in range(PARTS)], axis=0).T
            return carry

        lax.fori_loop(0, 16, one_tile, 0)
        results[half].start()

    def row_exchange():
        for d in range(1, 8):
            send(t1.at[r], t1.at[r], T1, t_sem.at[0], row_peers[d - 1])
        flip_out(0)
        arrive(t1.at[pl.ds(0, 7)], t_sem.at[0])
        t2[f] = jnp.sum(t1[...], axis=0)

    def layer_exchange():
        for d in range(1, 4):
            send(t2.at[f], t2.at[f], T2, t_sem.at[1], fib_peers[d - 1])
        flip_out(1)
        arrive(t2.at[pl.ds(0, 3)], t_sem.at[1])
        gain_ref[...] = total_rows / (jnp.sum(t2[...], axis=0) + epsilon)
        for copy in results:
            copy.wait()

    row_exchange()
    layer_exchange()
    left(t1.at[pl.ds(0, 7)], T1)
    left(t2.at[pl.ds(0, 3)], T2)


def on_device(a_tiles, a_cols, a_count, b_tiles, b_cols):
    block_rows = b_tiles.shape[0]
    total_rows = 8 * lax.axis_size("row") * TILE
    dma = pltpu.SemaphoreType.DMA
    any_ = pl.BlockSpec(memory_space=pl.ANY)
    squares, gains = pl.pallas_call(
        functools.partial(kernel, total_rows, lax.axis_size("fiber")),
        out_shape=(pltpu.VMEM((2, 16, TILE, TILE), F32), pltpu.VMEM((16, TILE), F32)),
        in_specs=[any_] * 5,
        out_specs=(any_, pl.BlockSpec(memory_space=pltpu.VMEM)),
        scratch_shapes=[
            pltpu.VMEM((8, 8, ASLOTS, TILE, TILE), jnp.bfloat16),
            *[pltpu.VMEM((512, WIDE, TILE), jnp.bfloat16)] * PARTS,
            pltpu.VMEM((64, TILE, TILE), jnp.bfloat16),
            pltpu.VMEM((8, 8, ASLOTS), jnp.int32),
            pltpu.VMEM((8, 1, 8), jnp.int32),
            pltpu.VMEM((8, 1, 64), jnp.int32),
            pltpu.VMEM((8, 8, TILE), jnp.int32),
            pltpu.SMEM((8, 8, TILE), jnp.int32),
            pltpu.VMEM((3 * PARTS, 1 + 8 * ASLOTS, WIDE, TILE), F32),
            pltpu.VMEM((6 * PARTS, 16, WIDE, TILE), jnp.int16),
            pltpu.VMEM((6 * PARTS, 4, TILE), F32),
            pltpu.VMEM((6 * PARTS, 16, WIDE, TILE), jnp.int16),
            pltpu.VMEM((6 * PARTS, 4, TILE), F32),
            pltpu.VMEM((2, PARTS, 16, WIDE, TILE), F32),
            pltpu.VMEM((2, 16, TILE, TILE), F32),
            pltpu.VMEM((8, 16, TILE), F32),
            pltpu.VMEM((4, 16, TILE), F32),
            dma((7 + PIECES,)),
            dma((22,)),
            dma((3,)),
            dma((8, 3)),
            dma((8, 2)),
            dma((8,)),
            dma((PARTS, PIECES, 2)),
            dma((PARTS, PIECES)),
            dma((PARTS,)),
            dma((2, 2, PARTS)),
            dma((2, PARTS)),
            dma((2,)),
        ],
        compiler_params=pltpu.CompilerParams(collective_id=0, has_side_effects=True, vmem_limit_bytes=56 * 1024 * 1024),
    )(a_cols, a_count.reshape(1, 8), b_cols.reshape(1, block_rows), a_tiles, b_tiles.reshape(block_rows, TILE, TILE))
    return squares * gains[None, :, None, :]


def solution(mesh):
    placed = (
        P("row", ("col", "fiber"), None, None),
        P("row", ("col", "fiber")),
        P("row", ("col", "fiber")),
        P(("row", "fiber"), "col", None, None),
        P(("row", "fiber"), "col"),
    )
    return jax.shard_map(
        on_device,
        mesh=mesh,
        in_specs=placed,
        out_specs=P(("row", "fiber"), "col", None, None),
        check_vma=False,
    )
```

```python
import functools

import jax
import jax.numpy as jnp
from jax import lax
from jax.experimental import pallas as pl
from jax.experimental.pallas import tpu as pltpu
from jax.sharding import PartitionSpec as P

MESH = pl.DeviceIdType.MESH
PT = 128
ASLOTS = 6
SLOTS8 = 8
TILE = 128
epsilon = 1e-06
F32 = jnp.float32
PIECES = 4
PARTS = 4
WIDE = TILE // PARTS
TOP = 32767.0


def kernel(total_rows, fibers, cols_ref, count_ref, target_ref, a_ref, b_ref, result_ref, gain_ref, pa, pb0, pb1, pb2, pb3, raw_b, ma, mn, mb, meta_v, meta_s, sums, cq_s, cs_s, cq_r, cs_r, own, out_ref,
           t1, t2, loc_sem, out_sem, m_sem, ao_sem, ap_sem, af_sem, bn_sem, bf_sem, kp_sem, far_sem, sum_sem, t_sem):
    r, c, f = lax.axis_index("row"), lax.axis_index("col"), lax.axis_index("fiber")
    x, k = r // 2, r % 2
    zl, y = c // 4, c % 4
    pb = (pb0, pb1, pb2, pb3)

    def rdev(rr):
        return (rr, c, f)

    def cdev(cc):
        return (r, cc, f)

    def fdev(ff):
        return (r, c, ff)

    def rid(dx, kk):
        return ((x + dx + 4) % 4) * 2 + kk

    def cid(dy, zz):
        return zz * 4 + (y + dy + 4) % 4

    XP, XM, KP = rdev(rid(1, k)), rdev(rid(-1, k)), rdev(rid(0, 1 - k))
    YP, YM, ZP = cdev(cid(1, zl)), cdev(cid(-1, zl)), cdev(cid(0, 1 - zl))
    plus, minus, far = (f + 3 + 2 * zl) % 4, (f + 1 + 2 * zl) % 4, (f + 2) % 4
    FP, FM = fdev(plus), fdev(minus)
    row_peers = [rdev((r + d) % 8) for d in range(1, 8)]
    col_peers = [cdev((c + d) % 8) for d in range(1, 8)]
    fib_peers = [fdev((f + d) % 4) for d in range(1, 4)]

    barrier = pltpu.get_barrier_semaphore()
    for peer in row_peers + col_peers + fib_peers:
        pl.semaphore_signal(barrier, inc=1, device_id=peer, device_id_type=MESH)

    piece = 64 // PIECES
    locals_ = [
        pltpu.make_async_copy(cols_ref, ma.at[c], loc_sem.at[0]),
        pltpu.make_async_copy(target_ref, mb.at[r], loc_sem.at[1]),
        pltpu.make_async_copy(a_ref, pa.at[:, c], loc_sem.at[2]),
    ]
    for q in range(PIECES):
        part = pl.ds(q * piece, piece)
        locals_.append(pltpu.make_async_copy(b_ref.at[part], raw_b.at[part], loc_sem.at[4 + q]))
    locals_.append(pltpu.make_async_copy(count_ref, mn.at[c], loc_sem.at[4 + PIECES]))
    for copy in locals_:
        copy.start()
    for q in range(3 * PARTS):
        sums[q, 0] = jnp.zeros((WIDE, TILE), F32)

    sum_set = (0, 0, 0, 0, 1, 2, 0, 1)

    def send(src, dst, out, into, device):
        pltpu.make_async_remote_copy(
            src_ref=src, dst_ref=dst, send_sem=out_sem.at[out], recv_sem=into, device_id=device, device_id_type=MESH
        ).start()

    def arrive(dst, into):
        pltpu.make_async_remote_copy(
            src_ref=dst, dst_ref=dst, send_sem=out_sem.at[0], recv_sem=into, device_id=KP, device_id_type=MESH
        ).wait_recv()

    def left(src, out):
        pltpu.make_async_remote_copy(
            src_ref=src, dst_ref=src, send_sem=out_sem.at[out], recv_sem=m_sem.at[0], device_id=KP, device_id_type=MESH
        ).wait_send()

    AO, AP, AF, CQ, CS, MA, MN, MB, T1, T2, BO, BK, BF = 0, 1, 2, 3, 4, 5, 6, 7, 8, 9, 10, 14, 18

    def flip_b(q):
        def one_tile(n, carry):
            tile = raw_b[n].T
            for h in range(PARTS):
                pb[h][r * 64 + n] = tile[h * WIDE : (h + 1) * WIDE]
            return carry

        locals_[3 + q].wait()
        lax.fori_loop(q * piece, (q + 1) * piece, one_tile, 0)

    def b_at(h, block, q):
        return pb[h].at[pl.ds(block * 64 + q * piece, piece)]

    def b_own(h, q):
        part = b_at(h, r, q)
        send(part, part, BO + h, bn_sem.at[h, q], XP)
        send(part, part, BO + h, bn_sem.at[h, q], XM)
        send(part, part, BO + h, kp_sem.at[h], KP)

    def b_all(h):
        for q in range(PIECES):
            b_own(h, q)

    def b_near(h, q):
        arrive(pb[h].at[pl.ds(0, 2 * piece)], bn_sem.at[h, q])
        up, down = b_at(h, rid(-1, k), q), b_at(h, rid(1, k), q)
        if q < PIECES // 2:
            send(up, up, BF + h, bf_sem.at[h, q], XP)
        else:
            send(down, down, BF + h, bf_sem.at[h, q - PIECES // 2], XM)
        send(up, up, BK + h, kp_sem.at[h], KP)
        send(down, down, BK + h, kp_sem.at[h], KP)

    def b_far(h, q):
        arrive(pb[h].at[pl.ds(0, 2 * piece)], bf_sem.at[h, q])
        for at in (q, q + PIECES // 2):
            part = b_at(h, rid(2, k), at)
            send(part, part, BK + h, kp_sem.at[h], KP)

    def b_done(h):
        arrive(pb[h].at[pl.ds(0, 256)], kp_sem.at[h])

    rows = [far * 2, far * 2 + 1, plus * 2 + 1, minus * 2, plus * 2, minus * 2 + 1, f * 2, f * 2 + 1]
    pair_rows = [far * 2, far * 2 + 1, minus * 2 + 1, plus * 2, minus * 2, plus * 2 + 1, f * 2, f * 2 + 1]

    def a_own(n, ways):
        for way, device in enumerate((ZP, YP, YM)):
            row = rows[n] if way else pair_rows[n]
            if way in ways:
                send(a_ref.at[row], pa.at[row, c], AO, ao_sem.at[n, min(way, 1)], device)

    def a_half(n, block, half, device):
        part = pa.at[rows[n], block, pl.ds(half * 3, 3)]
        send(part, part, AF, af_sem.at[n], device)

    def a_near(n):
        row = rows[n]
        block = cid(0, 1 - zl)
        arrive(pa.at[row, block], ao_sem.at[n, 0])
        for device in (YP, YM):
            send(pa.at[row, block], pa.at[row, block], AP, ap_sem.at[n], device)
        arrive(pa.at[row, pl.ds(0, 2)], ao_sem.at[n, 1])
        a_half(n, cid(-1, zl), 0, YP)
        a_half(n, cid(1, zl), 1, YM)
        if n < 2:
            for later in range(3 + n * 3, min(6 + n * 3, 8)):
                a_own(later, (0,))

    def a_pair(n):
        row = rows[n]
        arrive(pa.at[row, pl.ds(0, 2)], ap_sem.at[n])
        a_half(n, cid(-1, 1 - zl), 0, YP)
        a_half(n, cid(1, 1 - zl), 1, YM)
        if n + 2 < 8:
            a_own(n + 2, (1, 2))

    def a_done(n):
        arrive(pa.at[rows[n], pl.ds(0, 2)], af_sem.at[n])

    def block_of(o):
        return ((zl + o) % 2) * 4 + (y + o // 2 + 3) % 4

    def index_tables():
        for n, ref in enumerate((ma, mn, mb)):
            arrive(ref.at[pl.ds(0, 7)], m_sem.at[n])
        lane = lax.broadcasted_iota(jnp.int32, (64, TILE), 1)
        slot = lax.broadcasted_iota(jnp.int32, (64, TILE), 0)
        kept = slot - (SLOTS8 - ASLOTS) * (slot // SLOTS8) + 1
        lane6 = lax.broadcasted_iota(jnp.int32, (8, ASLOTS), 1)
        slot6 = lax.broadcasted_iota(jnp.int32, (8, ASLOTS), 0)
        lane_n = lax.broadcasted_iota(jnp.int32, (1, 8), 1)

        def one_row(i, carry):
            place = []
            for o in range(8):
                block = block_of(o)
                part = jnp.broadcast_to(ma[block, pl.ds(i, 1), :], (8, ASLOTS))
                part = jnp.sum(jnp.where(slot6 == lane6, part, 0), axis=1, keepdims=True)
                live = jnp.sum(jnp.where(lane_n == i, mn[block], 0), axis=1, keepdims=True)
                part = jnp.broadcast_to(part, (8, TILE))
                part = part // (64 * fibers) * 64 + part % 64
                live = slot[:8] < jnp.broadcast_to(live, (8, TILE))
                place.append(jnp.where(live, part, -1))
            place = jnp.concatenate(place, axis=0)
            target = jnp.zeros((64, 64), jnp.int32)
            for q in range(8):
                hit = place[:, :64] == lane[:, :64] + q * 64
                target = target + jnp.where(hit, mb[q] - c * 16 + 1, 0)
            target = jnp.sum(target, axis=1, keepdims=True)
            target = jnp.broadcast_to(target, (64, TILE))
            here = slot == lane
            target_l = jnp.sum(jnp.where(here, target, 0), axis=0, keepdims=True)
            place_l = jnp.sum(jnp.where(here, jnp.maximum(place, 0), 0), axis=0, keepdims=True)
            same = (target == target_l) & (slot < lane) & (target > 0)
            prev = jnp.max(jnp.where(same, kept, 0), axis=0, keepdims=True)
            last = jnp.max(jnp.where(target == lane + 1, kept, 0), axis=0, keepdims=True)
            meta_v[i, 0:1, :] = place_l
            meta_v[i, 1:2, :] = prev
            meta_v[i, 2:3, :] = last
            return carry

        lax.fori_loop(0, 8, one_row, 0)
        copy = pltpu.make_async_copy(meta_v, meta_s, loc_sem.at[3])
        copy.start()
        copy.wait()
        locals_[2].wait()

    def products(n, parts, first=0, stop=8):
        row = rows[n]
        into = PARTS * sum_set[n]

        def one_block(o, carry):
            block = block_of(o)
            for e in range(ASLOTS):
                t = o * SLOTS8 + e
                place, prev = meta_s[row, 0, t], meta_s[row, 1, t]
                left = jnp.concatenate([pb[h][place] for h in parts], axis=0)
                product = lax.dot_general(left, pa[row, block, e], (((1,), (1,)), ((), ())), preferred_element_type=F32)
                for n_h, h in enumerate(parts):
                    sums[into + h, 1 + o * ASLOTS + e] = product[n_h * WIDE : (n_h + 1) * WIDE] + sums[into + h, prev]
            return carry

        lax.fori_loop(first, stop, one_block, 0, unroll=4 if stop - first == 8 else 2)

    wide_lane = lax.broadcasted_iota(jnp.int32, (WIDE, TILE), 1)
    wide_slot = lax.broadcasted_iota(jnp.int32, (WIDE, TILE), 0)

    def to_lanes(column, i):
        return jnp.sum(jnp.where(wide_lane == wide_slot + i * WIDE, column, 0.0), axis=0, keepdims=True)

    def to_column(row, i):
        return jnp.sum(jnp.where(wide_lane == wide_slot + i * WIDE, row, 0.0), axis=1, keepdims=True)

    def decoded(at, g, i):
        return cq_r[at, g * 4 + i].astype(jnp.int32).astype(F32) * to_column(cs_r[at, pl.ds(g, 1), :], i)

    def emit(n, h, at, device, add=None):
        row = rows[n]
        slot = at
        at = h * 6 + at

        def four_tiles(g, carry):
            scales = jnp.zeros((1, TILE), F32)
            for i in range(4):
                value = sums[PARTS * sum_set[n] + h, meta_s[row, 2, g * 4 + i]]
                if add is not None:
                    value = value + decoded(h * 6 + add, g, i)
                top = jnp.max(jnp.abs(value), axis=1, keepdims=True)
                gain = jnp.where(top > 1e-30, TOP / jnp.maximum(top, 1e-30), 0.0)
                cq_s[at, g * 4 + i] = jnp.floor(value * gain + 0.5).astype(jnp.int32).astype(jnp.int16)
                scales = scales + to_lanes(top * (1.0 / TOP), i)
            cs_s[at, pl.ds(g, 1), :] = scales
            return carry

        lax.fori_loop(0, 4, four_tiles, 0)
        into = [far_sem.at[n, slot, h] if slot < 2 else sum_sem.at[n, h] for n in range(2)]
        send(cs_s.at[at], cs_r.at[at], CS, into[0], device)
        send(cq_s.at[at], cq_r.at[at], CQ, into[1], device)

    def c_arrive(at, h):
        arrive(cs_r.at[h * 6 + at], far_sem.at[0, at, h])
        arrive(cq_r.at[h * 6 + at], far_sem.at[1, at, h])

    def gather(h):
        arrive(cs_r.at[pl.ds(h * 6 + 2, 4)], sum_sem.at[0, h])
        arrive(cq_r.at[pl.ds(h * 6 + 2, 4)], sum_sem.at[1, h])

        def four_tiles(g, carry):
            for i in range(4):
                for half in range(2):
                    own[half, h, g * 4 + i] = decoded(h * 6 + 2 + half, g, i) + decoded(h * 6 + 4 + half, g, i)
            return carry

        lax.fori_loop(0, 4, four_tiles, 0)

    def finish(n, h):
        row = rows[n]

        def four_tiles(g, carry):
            for i in range(4):
                j = g * 4 + i
                value = own[n - 6, h, j] + sums[PARTS * sum_set[n] + h, meta_s[row, 2, j]]
                value = value * value
                own[n - 6, h, j] = value
                total = to_lanes(jnp.sum(value, axis=1, keepdims=True), h)
                if (n, h) != (6, 0):
                    total = total + t1[r, pl.ds(j, 1), :]
                t1[r, pl.ds(j, 1), :] = total
            return carry

        lax.fori_loop(0, 4, four_tiles, 0)

    def finish_last(h):
        arrive(cs_r.at[pl.ds(h * 6 + 2, 4)], sum_sem.at[0, h])
        arrive(cq_r.at[pl.ds(h * 6 + 2, 4)], sum_sem.at[1, h])

        def four_tiles(g, carry):
            for i in range(4):
                j = g * 4 + i
                total = jnp.zeros((WIDE, TILE), F32)
                for half in range(2):
                    value = decoded(h * 6 + 2 + half, g, i) + decoded(h * 6 + 4 + half, g, i)
                    value = value + sums[PARTS * sum_set[6 + half] + h, meta_s[rows[6 + half], 2, j]]
                    value = value * value
                    own[half, h, j] = value
                    total = total + value
                total = to_lanes(jnp.sum(total, axis=1, keepdims=True), h)
                t1[r, pl.ds(j, 1), :] = t1[r, pl.ds(j, 1), :] + total
            return carry

        lax.fori_loop(0, 4, four_tiles, 0)

    slots = ((0, FP, None), (1, FM, None), (3, FP, None), (4, FM, None), (2, FP, 0), (5, FM, 1))

    def give(n, h):
        at, device, add = slots[n]
        if h == PARTS - 1:
            device = FP if n == 1 else device
            add = {2: 1, 5: None}.get(n, add)
        if add is not None:
            c_arrive(add, h)
        emit(n, h, at, device, add)

    def unit(n, *parts):
        products(n, parts)
        for h in parts:
            give(n, h)

    every = tuple(range(PARTS))

    def start():
        flip_b(0)
        pl.semaphore_wait(barrier, len(row_peers) + len(col_peers) + len(fib_peers))
        a_own(0, (0, 1, 2))
        b_own(0, 0)
        for n in (0, 1, -1):
            locals_[n].wait()
        for d in range(1, 8):
            send(ma.at[c], ma.at[c], MA, m_sem.at[0], col_peers[d - 1])
            send(mn.at[c], mn.at[c], MN, m_sem.at[1], col_peers[d - 1])
            send(mb.at[r], mb.at[r], MB, m_sem.at[2], row_peers[d - 1])

    def start_b():
        flip_b(1)
        b_own(0, 1)
        a_own(1, (0, 1, 2))
        flip_b(2)
        b_own(0, 2)
        a_own(2, (0,))
        flip_b(3)
        b_own(0, 3)

    def last_waits():
        left(pa.at[pl.ds(0, 3)], AO)
        left(pa.at[pl.ds(0, 2)], AP)
        left(pa.at[pl.ds(0, 2)], AF)
        left(cq_s, CQ)
        left(cs_s, CS)
        left(ma.at[pl.ds(0, 7)], MA)
        left(mn.at[pl.ds(0, 7)], MN)
        left(mb.at[pl.ds(0, 7)], MB)
        for h in range(PARTS):
            left(pb[h].at[pl.ds(0, 192)], BO + h)
            left(pb[h].at[pl.ds(0, 192)], BK + h)
            left(pb[h].at[pl.ds(0, 64)], BF + h)

    start()
    start_b()
    b_near(0, 0)
    a_near(0)
    b_near(0, 1)
    index_tables()
    b_near(0, 2)
    b_near(0, 3)
    b_all(1)
    a_pair(0)
    a_near(1)
    b_far(0, 0)
    b_far(0, 1)
    b_done(0)
    a_done(0)
    unit(0, 0)
    b_near(1, 0)
    b_near(1, 1)
    b_near(1, 2)
    a_pair(1)
    a_near(2)
    b_near(1, 3)
    b_all(2)
    a_done(1)
    unit(1, 0)
    b_far(1, 0)
    b_far(1, 1)
    b_done(1)
    unit(0, 1)
    b_near(2, 0)
    a_pair(2)
    a_near(3)
    unit(1, 1)
    b_near(2, 1)
    b_near(2, 2)
    a_done(2)
    unit(2, 0, 1)
    b_near(2, 3)
    b_all(3)
    b_far(2, 0)
    a_pair(3)
    a_near(4)
    b_far(2, 1)
    b_done(2)
    unit(1, 2)
    unit(0, 2)
    b_near(3, 0)
    b_near(3, 1)
    a_done(3)
    unit(3, 0, 1)
    b_near(3, 2)
    unit(2, 2)
    b_near(3, 3)
    unit(3, 2)
    a_pair(4)
    a_near(5)
    b_far(3, 0)
    b_far(3, 1)
    a_done(4)
    products(4, (0, 1, 2))
    give(4, 0)
    b_done(3)
    unit(1, 3)
    unit(0, 3)
    give(4, 1)
    a_pair(5)
    a_near(6)
    give(4, 2)
    unit(3, 3)
    products(4, (3,))
    a_done(5)
    products(5, every)
    give(5, 0)
    give(5, 1)
    give(5, 2)
    give(5, 3)
    unit(2, 3)
    give(4, 3)
    a_pair(6)
    a_near(7)
    products(6, every, 0, 6)
    a_done(6)
    products(6, every, 6, 8)
    a_pair(7)
    products(7, every, 0, 6)
    gather(0)
    finish(6, 0)
    gather(1)
    finish(6, 1)
    a_done(7)
    products(7, every, 6, 8)
    finish(7, 0)
    finish(7, 1)
    gather(2)
    finish(6, 2)
    finish(7, 2)
    last_waits()
    finish_last(3)

    results = [pltpu.make_async_copy(out_ref.at[half], result_ref.at[half], loc_sem.at[5 + PIECES + half]) for half in range(2)]

    def flip_out(half):
        def one_tile(j, carry):
            out_ref[half, j] = jnp.concatenate([own[half, h, j] for h in range(PARTS)], axis=0).T
            return carry

        lax.fori_loop(0, 16, one_tile, 0)
        results[half].start()

    def row_exchange():
        for d in range(1, 8):
            send(t1.at[r], t1.at[r], T1, t_sem.at[0], row_peers[d - 1])
        flip_out(0)
        arrive(t1.at[pl.ds(0, 7)], t_sem.at[0])
        t2[f] = jnp.sum(t1[...], axis=0)

    def layer_exchange():
        for d in range(1, 4):
            send(t2.at[f], t2.at[f], T2, t_sem.at[1], fib_peers[d - 1])
        flip_out(1)
        arrive(t2.at[pl.ds(0, 3)], t_sem.at[1])
        gain_ref[...] = total_rows / (jnp.sum(t2[...], axis=0) + epsilon)
        for copy in results:
            copy.wait()

    row_exchange()
    layer_exchange()
    left(t1.at[pl.ds(0, 7)], T1)
    left(t2.at[pl.ds(0, 3)], T2)


def on_device(a_tiles, a_cols, a_count, b_tiles, b_cols):
    block_rows = b_tiles.shape[0]
    total_rows = 8 * lax.axis_size("row") * TILE
    dma = pltpu.SemaphoreType.DMA
    any_ = pl.BlockSpec(memory_space=pl.ANY)
    squares, gains = pl.pallas_call(
        functools.partial(kernel, total_rows, lax.axis_size("fiber")),
        out_shape=(pltpu.VMEM((2, 16, TILE, TILE), F32), pltpu.VMEM((16, TILE), F32)),
        in_specs=[any_] * 5,
        out_specs=(any_, pl.BlockSpec(memory_space=pltpu.VMEM)),
        scratch_shapes=[
            pltpu.VMEM((8, 8, ASLOTS, TILE, TILE), jnp.bfloat16),
            *[pltpu.VMEM((512, WIDE, TILE), jnp.bfloat16)] * PARTS,
            pltpu.VMEM((64, TILE, TILE), jnp.bfloat16),
            pltpu.VMEM((8, 8, ASLOTS), jnp.int32),
            pltpu.VMEM((8, 1, 8), jnp.int32),
            pltpu.VMEM((8, 1, 64), jnp.int32),
            pltpu.VMEM((8, 8, TILE), jnp.int32),
            pltpu.SMEM((8, 8, TILE), jnp.int32),
            pltpu.VMEM((3 * PARTS, 1 + 8 * ASLOTS, WIDE, TILE), F32),
            pltpu.VMEM((6 * PARTS, 16, WIDE, TILE), jnp.int16),
            pltpu.VMEM((6 * PARTS, 4, TILE), F32),
            pltpu.VMEM((6 * PARTS, 16, WIDE, TILE), jnp.int16),
            pltpu.VMEM((6 * PARTS, 4, TILE), F32),
            pltpu.VMEM((2, PARTS, 16, WIDE, TILE), F32),
            pltpu.VMEM((2, 16, TILE, TILE), F32),
            pltpu.VMEM((8, 16, TILE), F32),
            pltpu.VMEM((4, 16, TILE), F32),
            dma((7 + PIECES,)),
            dma((22,)),
            dma((3,)),
            dma((8, 2)),
            dma((8,)),
            dma((8,)),
            dma((PARTS, PIECES)),
            dma((PARTS, PIECES // 2)),
            dma((PARTS,)),
            dma((2, 2, PARTS)),
            dma((2, PARTS)),
            dma((2,)),
        ],
        compiler_params=pltpu.CompilerParams(collective_id=0, has_side_effects=True, vmem_limit_bytes=56 * 1024 * 1024),
    )(a_cols, a_count.reshape(1, 8), b_cols.reshape(1, block_rows), a_tiles, b_tiles.reshape(block_rows, TILE, TILE))
    return squares * gains[None, :, None, :]


def solution(mesh):
    placed = (
        P("row", ("col", "fiber"), None, None),
        P("row", ("col", "fiber")),
        P("row", ("col", "fiber")),
        P(("row", "fiber"), "col", None, None),
        P(("row", "fiber"), "col"),
    )
    return jax.shard_map(
        on_device,
        mesh=mesh,
        in_specs=placed,
        out_specs=P(("row", "fiber"), "col", None, None),
        check_vma=False,
    )
```
